128 devices in a mesh: dp: 8 (over z, core), seq: 16 (over x, y).
Axes of the slice: x: 4, y: 4, z: 4, core: 2. Of those that a mesh axis runs over, the one named last changes fastest.
Arguments:
- q_proj: bfloat16 [16384, 8192], P(('dp', 'seq')), may hold values from -6 to 6
- k_proj: bfloat16 [16384, 1024], P(('dp', 'seq')), may hold values from -6 to 6
- v_proj: bfloat16 [16384, 1024], P(('dp', 'seq')), may hold values from -6 to 6
- q_gain: float32 [128], replicated, may hold values from 0.5 to 6
- k_gain: float32 [128], replicated, may hold values from 0.5 to 6
- dout: bfloat16 [16384, 8192], P(('dp', 'seq')), may hold values from -7 to 7
- segments: int32 [16384], replicated, may hold values from 0 to 7, as said below
Outputs:
- attn_out: bfloat16 [16384, 8192], P(('dp', 'seq'))
- q_grad: bfloat16 [16384, 8192], P(('dp', 'seq'))
- k_grad: bfloat16 [16384, 1024], P(('dp', 'seq'))
- v_grad: bfloat16 [16384, 1024], P(('dp', 'seq'))
- q_gain_grad: float32 [128], replicated
- k_gain_grad: float32 [128], replicated
The draws below stay inside these ranges and needn't reach their ends.
Inputs may be any that keep to these rules, and one draw needn't show every extreme that they name: `segments`: along each packed row of 2048 tokens the ids never fall and start at 0; of the two rows 2i and 2i + 1 one holds a single rollout filling the row and the other exactly 8 rollouts.
All inputs are finite; a program needn't handle non-finite values.
Results may differ from the reference program's by a relative error of at most 0.017.
The reference program's roundings to bfloat16 on the way (of `q_norm`, `k_norm`, `probs` and `dscore`) count: a program that leaves them out, or rounds other values in their place, can miss the bound.
Values may be sent and summed in bfloat16 or wider, within the bound.
A program may use at most 192 MiB of HBM per device.

```python
import math
import jax
import jax.numpy as jnp
from jax import lax

QH = 64
KVH = 8
HD = 128
SEQ_LEN = 2048
TOKENS = 16384
PIECES = 8


def key_base(key):
    return jax.random.truncated_normal(key, -5.0, 5.0, (TOKENS, KVH, HD), jnp.float32)


def draw_k_proj(key, part):
    base = key_base(key)
    return base.reshape(TOKENS, KVH * HD).astype(jnp.bfloat16)


def draw_q_proj(key, part):
    key = jax.random.fold_in(key, 5)
    own = jax.random.truncated_normal(key, -5.0, 5.0, (TOKENS, QH, HD), jnp.float32)
    return own.reshape(TOKENS, QH * HD).astype(jnp.bfloat16)


def gain_values(key):
    return jnp.exp(jax.random.uniform(key, (HD,), jnp.float32, jnp.log(0.5), jnp.log(2.0)))


def draw_q_gain(key, part):
    key = jax.random.fold_in(key, 17)
    return gain_values(key)


def draw_k_gain(key, part):
    key = jax.random.fold_in(key, 19)
    return gain_values(key)


def draw_dout(key, part):
    key = jax.random.fold_in(key, 23)
    first = jax.random.fold_in(key, 0)
    noise = jax.random.truncated_normal(first, -3.0, 3.0, (TOKENS, QH * HD), jnp.float32)
    rising = 0.5 + jnp.arange(TOKENS, dtype=jnp.int32).astype(jnp.float32) / TOKENS
    values = noise * rising[:, None]
    return values.astype(jnp.bfloat16)


def draw_segments(key, part):
    key = jax.random.fold_in(key, 29)
    first, second = jax.random.split(key)
    rows = TOKENS // SEQ_LEN
    pieces = PIECES
    heavy_pick = jax.random.randint(first, (rows // 2,), 0, 2)
    row_index = jnp.arange(rows, dtype=jnp.int32)
    heavy = row_index % 2 == heavy_pick[row_index // 2]
    inner = jnp.arange(SEQ_LEN - 1, dtype=jnp.int32)
    scores = jax.random.randint(second, (rows, SEQ_LEN - 1), 0, 2 ** 15) * SEQ_LEN + inner[None, :]
    order = jnp.argsort(scores, axis=1, stable=True).astype(jnp.int32)
    chosen = order[:, :pieces - 1] + 1
    column = jnp.arange(SEQ_LEN, dtype=jnp.int32)
    starts = jnp.any(chosen[:, :, None] == column[None, None, :], axis=1)
    ids = jnp.cumsum(starts.astype(jnp.int32), axis=1)
    ids = jnp.where(heavy[:, None], 0, ids)
    return ids.reshape(TOKENS).astype(jnp.int32)


def block_scale(own_key, shape, cuts, smallest, high):
    level = 1.0
    for position, parts in cuts:
        draws = jax.random.uniform(jax.random.fold_in(jax.random.fold_in(own_key, 6), position), (parts,), jnp.float32, smallest / len(cuts), high / len(cuts))
        level = level * jnp.repeat(jnp.exp(draws), shape[position] // parts).reshape((-1,) + (1,) * (len(shape) - 1 - position))
    return level


def normal_values(stream_key, shape, spread, reach, shards=(), kind=jnp.bfloat16):
    drawn = jax.random.normal(stream_key, shape, jnp.float32) * spread
    if len(shards) > 0:
        drawn = block_scale(stream_key, shape, shards, -0.22, 0.18) * drawn
    return jnp.clip(drawn, min=-reach, max=reach).astype(kind)


def setup_inputs(seed: int = 0) -> dict:
    arg_keys = jax.random.split(jax.random.key(seed), 8)
    return {
        "q_proj": draw_q_proj(jax.random.fold_in(arg_keys[7], 71), 0),
        "k_proj": draw_k_proj(jax.random.fold_in(arg_keys[7], 71), 0),
        "v_proj": normal_values(arg_keys[2], (TOKENS, KVH * HD), 1.0, 6.0, ((0, 128),)),
        "q_gain": draw_q_gain(jax.random.fold_in(arg_keys[7], 71), 0),
        "k_gain": draw_k_gain(jax.random.fold_in(arg_keys[7], 71), 0),
        "dout": draw_dout(jax.random.fold_in(arg_keys[7], 71), 0),
        "segments": draw_segments(jax.random.fold_in(arg_keys[7], 71), 0),
    }


tile_span = 512
neg_fill = -1e+30
norm_eps = 1e-06

def tile_scores(q_part, keys, key_ids, ids_part, positions, kblock, k_tile, scale):
    k_part = lax.dynamic_slice_in_dim(keys, kblock * k_tile, k_tile, 0)
    ids_key = lax.dynamic_slice_in_dim(key_ids, kblock * k_tile, k_tile, 0)
    key_pos = kblock * k_tile + jnp.arange(k_tile, dtype=jnp.int32)
    allowed = (ids_part[:, None] == ids_key[None, :]) & (key_pos[None, :] <= positions[:, None])
    allowed = allowed[:, None, None, :]
    scores = jnp.einsum('qgrd,kgd->qgrk', q_part, k_part, preferred_element_type=jnp.float32) * scale
    return (jnp.where(allowed, scores, neg_fill), allowed)

def tile_live(key_ids, ids_part, positions, kblock, k_tile):
    first_key = kblock * k_tile
    last_id = lax.dynamic_index_in_dim(key_ids, first_key + k_tile - 1, 0, keepdims=False)
    return (first_key <= positions[-1]) & (last_id >= ids_part[0])

def attend(queries, keys, values, upstream, query_ids, key_ids, query_start):
    q_len, groups, ratio, head_dim = queries.shape
    k_len = keys.shape[0]
    q_tile = min(tile_span, q_len)
    k_tile = min(tile_span, k_len)
    k_count = k_len // k_tile
    scale = 1.0 / math.sqrt(head_dim)
    key_grad = jnp.zeros((k_len, groups, head_dim), jnp.float32)
    value_grad = jnp.zeros((k_len, groups, head_dim), jnp.float32)
    outputs = []
    query_grads = []
    for block in range(q_len // q_tile):
        q_part = queries[block * q_tile:(block + 1) * q_tile]
        g_part = upstream[block * q_tile:(block + 1) * q_tile]
        ids_part = query_ids[block * q_tile:(block + 1) * q_tile]
        positions = query_start + block * q_tile + jnp.arange(q_tile, dtype=jnp.int32)

        def stat_step(kblock, carry):

            def update(state):
                top, total = state
                masked, allowed = tile_scores(q_part, keys, key_ids, ids_part, positions, kblock, k_tile, scale)
                new_top = jnp.maximum(top, lax.optimization_barrier(jnp.max(masked, axis=-1)))
                weights = jnp.where(allowed, jnp.exp(masked - new_top[..., None]), 0.0)
                return (new_top, total * jnp.exp(top - new_top) + lax.optimization_barrier(jnp.sum(weights, axis=-1)))
            return lax.cond(tile_live(key_ids, ids_part, positions, kblock, k_tile), update, lambda state: state, carry)
        start_top = jnp.full((q_tile, groups, ratio), neg_fill, jnp.float32)
        start_total = jnp.zeros((q_tile, groups, ratio), jnp.float32)
        top, total = lax.fori_loop(jnp.int32(0), jnp.int32(k_count), stat_step, (start_top, start_total))
        logsum = top + jnp.log(total)

        def out_step(kblock, carry):

            def update(accum):
                masked, allowed = tile_scores(q_part, keys, key_ids, ids_part, positions, kblock, k_tile, scale)
                v_part = lax.dynamic_slice_in_dim(values, kblock * k_tile, k_tile, 0)
                probs = jnp.exp(masked - logsum[..., None]).astype(jnp.bfloat16)
                return accum + jnp.einsum('qgrk,kgd->qgrd', probs, v_part, preferred_element_type=jnp.float32)
            return lax.cond(tile_live(key_ids, ids_part, positions, kblock, k_tile), update, lambda accum: accum, carry)
        accum = lax.fori_loop(jnp.int32(0), jnp.int32(k_count), out_step, jnp.zeros((q_tile, groups, ratio, head_dim), jnp.float32))
        out_part = accum.astype(jnp.bfloat16)
        delta = lax.optimization_barrier(jnp.sum(g_part.astype(jnp.float32) * out_part.astype(jnp.float32), axis=-1))

        def grad_step(kblock, carry):

            def update(state):
                q_acc, k_acc, v_acc = state
                masked, allowed = tile_scores(q_part, keys, key_ids, ids_part, positions, kblock, k_tile, scale)
                k_part = lax.dynamic_slice_in_dim(keys, kblock * k_tile, k_tile, 0)
                v_part = lax.dynamic_slice_in_dim(values, kblock * k_tile, k_tile, 0)
                exact = jnp.exp(masked - logsum[..., None])
                probs = exact.astype(jnp.bfloat16)
                dprob = jnp.einsum('qgrd,kgd->qgrk', g_part, v_part, preferred_element_type=jnp.float32)
                dscore = (exact * (dprob - delta[..., None]) * scale).astype(jnp.bfloat16)
                q_acc = q_acc + jnp.einsum('qgrk,kgd->qgrd', dscore, k_part, preferred_element_type=jnp.float32)
                k_tile_grad = jnp.einsum('qgrk,qgrd->kgd', dscore, q_part, preferred_element_type=jnp.float32)
                v_tile_grad = jnp.einsum('qgrk,qgrd->kgd', probs, g_part, preferred_element_type=jnp.float32)
                first_key = kblock * k_tile
                k_acc = lax.dynamic_update_slice_in_dim(k_acc, lax.dynamic_slice_in_dim(k_acc, first_key, k_tile, 0) + k_tile_grad, first_key, 0)
                v_acc = lax.dynamic_update_slice_in_dim(v_acc, lax.dynamic_slice_in_dim(v_acc, first_key, k_tile, 0) + v_tile_grad, first_key, 0)
                return (q_acc, k_acc, v_acc)
            return lax.cond(tile_live(key_ids, ids_part, positions, kblock, k_tile), update, lambda state: state, carry)
        start_q = jnp.zeros((q_tile, groups, ratio, head_dim), jnp.float32)
        q_acc, key_grad, value_grad = lax.fori_loop(jnp.int32(0), jnp.int32(k_count), grad_step, (start_q, key_grad, value_grad))
        outputs.append(out_part)
        query_grads.append(q_acc)
    return (jnp.concatenate(outputs, axis=0), jnp.concatenate(query_grads, axis=0), key_grad, value_grad)

def normalize(raw, gain):
    inverse = lax.rsqrt(lax.optimization_barrier(jnp.mean(raw * raw, axis=-1, keepdims=True)) + norm_eps)
    hatted = raw * inverse
    return (hatted, inverse, (hatted * gain).astype(jnp.bfloat16))

def norm_backward(grad_norm, hatted, inverse, gain):
    scaled = grad_norm * gain
    return (inverse * (scaled - hatted * lax.optimization_barrier(jnp.mean(scaled * hatted, axis=-1, keepdims=True)))).astype(jnp.bfloat16)

def reference(q_proj, k_proj, v_proj, q_gain, k_gain, dout, segments):
    ratio = QH // KVH
    rows = TOKENS // SEQ_LEN
    q_hat, q_inv, q_norm = normalize(q_proj.reshape(TOKENS, QH, HD).astype(jnp.float32), q_gain)
    k_hat, k_inv, k_norm = normalize(k_proj.reshape(TOKENS, KVH, HD).astype(jnp.float32), k_gain)
    items = (q_norm.reshape(rows, SEQ_LEN, KVH, ratio, HD), k_norm.reshape(rows, SEQ_LEN, KVH, HD), v_proj.reshape(rows, SEQ_LEN, KVH, HD), dout.reshape(rows, SEQ_LEN, KVH, ratio, HD), segments.reshape(rows, SEQ_LEN))

    def per_row(item):
        return attend(item[0], item[1], item[2], item[3], item[4], item[4], 0)
    outputs, q_norm_grad, k_norm_grad, v_sum = lax.map(per_row, items)
    q_norm_grad = q_norm_grad.reshape(TOKENS, QH, HD)
    k_norm_grad = k_norm_grad.reshape(TOKENS, KVH, HD)
    q_grad = norm_backward(q_norm_grad, q_hat, q_inv, q_gain)
    k_grad = norm_backward(k_norm_grad, k_hat, k_inv, k_gain)
    q_gain_grad = lax.optimization_barrier(jnp.sum(q_norm_grad * q_hat, axis=(0, 1))) / math.sqrt(TOKENS * QH)
    k_gain_grad = lax.optimization_barrier(jnp.sum(k_norm_grad * k_hat, axis=(0, 1))) / math.sqrt(TOKENS * KVH)
    return (outputs.reshape(TOKENS, QH * HD), q_grad.reshape(TOKENS, QH * HD), k_grad.reshape(TOKENS, KVH * HD), v_sum.astype(jnp.bfloat16).reshape(TOKENS, KVH * HD), q_gain_grad, k_gain_grad)
```

```python
import math

import jax
import jax.numpy as jnp
from jax import lax
from jax.experimental import pallas as pl
from jax.experimental.pallas import tpu as pltpu
from jax.sharding import PartitionSpec as P

QH = 64
KVH = 8
HD = 128
EPS = 1e-06
NEG = -1e30
MESH = pl.DeviceIdType.MESH
BLK = 128
SIDE = 4
PART = 4096
OWN = 1024
CH = 512
KT = 256
SCALE = 1.0 / math.sqrt(HD)
LOG2E = math.log2(math.e)
bf16 = jnp.bfloat16
f32 = jnp.float32


def dot_nt(a, b):
    return lax.dot_general(a, b, (((1,), (1,)), ((), ())), preferred_element_type=f32)


def dot_nn(a, b):
    return lax.dot_general(a, b, (((1,), (0,)), ((), ())), preferred_element_type=f32)


def fold(x, op):
    rows, cols = x.shape
    return op(x.reshape(rows // 8, 8, cols), axis=0)


def kernel(
    q, k, v, do, seg, qg, kg,
    o, dq, dk, dv, qgp, kgp,
    qs, ds_, kv, kn, vn, kt_, vt_, os_, dqs, es, ms, firsts, dka, dva, sb, rb, fb, qn, ot, dqt, gacc,
    s_in, r_in, s_kv, r_kv, s_ag, r_ag, s_out, r_out, s_rs, r_rs, s_f, r_f,
):
    seq = lax.axis_index("seq")
    dp = lax.axis_index("dp")
    x, y = seq // SIDE, seq % SIDE
    mine = (x, y)

    def where(p, j):
        return (dp, lax.select(p == 0, j * SIDE + y, x * SIDE + j))

    def own(p):
        return lax.select(p == 0, x, y)

    def remote(src, dst, ss, rs, dev):
        return pltpu.make_async_remote_copy(
            src_ref=src, dst_ref=dst, send_sem=ss, recv_sem=rs, device_id=dev, device_id_type=MESH
        )

    def cols(start, width):
        return pl.ds(pl.multiple_of(start, width), width)

    barrier = pltpu.get_barrier_semaphore()
    for p in (0, 1):
        for d in (1, 2, 3):
            j = (mine[p] + d) % SIDE
            dev = (dp, j * SIDE + y) if p == 0 else (dp, x * SIDE + j)
            pl.semaphore_signal(barrier, inc=1, device_id=dev, device_id_type=MESH)

    for p in (0, 1):
        me = mine[p]
        for i, src in enumerate((k, v)):
            pltpu.make_async_copy(
                src.at[:, cols(p * 512 + me * HD, HD)], kv.at[p, i, x, y], r_kv.at[p, i, me]
            ).start()
    pl.semaphore_wait(barrier, 6)

    def dev_of(p, j):
        return (dp, j * SIDE + y) if p == 0 else (dp, x * SIDE + j)

    kv_sends = []
    for d in (1, 3, 2):
        for p in (0, 1):
            me = mine[p]
            j = (me + d) % SIDE
            for i, src in enumerate((k, v)):
                c = remote(
                    src.at[:, cols(p * 512 + j * HD, HD)], kv.at[p, i, x, y],
                    s_kv.at[p, i, d], r_kv.at[p, i, me], dev_of(p, j),
                )
                c.start()
                kv_sends.append(c)

    for p in (0, 1):
        me = mine[p]
        for i, src in enumerate((q, do)):
            dst = (qs, ds_)[i]
            for c in (0, 1):
                pltpu.make_async_copy(
                    src.at[:, cols(p * PART + me * OWN + c * CH, CH)],
                    dst.at[p, me, c], r_in.at[i, p, me, c],
                ).start()

    ag_sends = []
    for p in (0, 1):
        me = mine[p]
        other = mine[1 - p]
        for j in range(SIDE):
            for i in (0, 1):
                blk = kv.at[p, i, j, y] if p == 0 else kv.at[p, i, x, j]
                pltpu.make_async_copy(blk, blk, r_kv.at[p, i, j]).wait()
        held = kv.at[0, :, :, y] if p == 0 else kv.at[1, :, x]
        for d in (1, 3, 2):
            c = remote(
                held, held, s_ag.at[p, d], r_ag.at[p, other], dev_of(1 - p, (other + d) % SIDE)
            )
            c.start()
            ag_sends.append(c)

    in_sends = []
    for c in (0, 1):
        for d in (1, 3, 2):
            for p in (0, 1):
                me = mine[p]
                j = (me + d) % SIDE
                for i, src in enumerate((q, do)):
                    dst = (qs, ds_)[i]
                    cp = remote(
                        src.at[:, cols(p * PART + j * OWN + c * CH, CH)], dst.at[p, me, c],
                        s_in.at[i, p, d, c], r_in.at[i, p, me, c], dev_of(p, j),
                    )
                    cp.start()
                    in_sends.append(cp)

    ids = seg[...]
    first = jnp.zeros((16, BLK), jnp.int32)
    for value in range(7):
        hits = jnp.where(ids == value, 1, 0)
        count = jnp.sum(jnp.sum(hits, axis=1, keepdims=True), axis=0, keepdims=True)
        first = first + jnp.where(ids > value, count, 0)
    seg_first = first

    dka[...] = jnp.zeros_like(dka)
    dva[...] = jnp.zeros_like(dva)
    gacc[...] = jnp.zeros_like(gacc)
    for i in range(16):
        firsts[i] = seg_first[i : i + 1, :]

    for p in (0, 1):
        other = mine[1 - p]
        for d in (1, 3, 2):
            j = (other + d) % SIDE
            blk = kv.at[0, :, :, j] if p == 0 else kv.at[1, :, j]
            pltpu.make_async_copy(blk, blk, r_ag.at[p, j]).wait()

    def prep(t, carry):
        p, b = t // 16, t % 16
        raw = kv[p, 0, b // SIDE, b % SIDE].astype(f32)
        inv = lax.rsqrt(jnp.mean(raw * raw, axis=-1, keepdims=True) + EPS)
        normed = (raw * inv * kg[...]).astype(bf16)
        rows = cols(b * BLK, BLK)
        kn[p, rows, :] = normed
        kt_[p, :, rows] = normed.astype(f32).T.astype(bf16)
        val = kv[p, 1, b // SIDE, b % SIDE]
        vn[p, rows, :] = val
        vt_[p, :, rows] = val.astype(f32).T.astype(bf16)
        return carry

    lax.fori_loop(0, 32, prep, 0)

    def unit(u, carry):
        c = u // 8
        p = u % 2
        step = (u % 8) // 2
        d = lax.select(step == 2, 3, lax.select(step == 3, 2, step))
        me = own(p)
        j = (me + d) % SIDE
        b = lax.select(p == 0, j * SIDE + y, x * SIDE + j)
        n_tiles = b // 2 + 1
        for i, dst in enumerate((qs, ds_)):
            blk = dst.at[p, j, c]
            pltpu.make_async_copy(blk, blk, r_in.at[i, p, j, c]).wait()

        for h in range(4):
            raw = qs[p, j, c, :, h * HD : (h + 1) * HD].astype(f32)
            inv = lax.rsqrt(jnp.mean(raw * raw, axis=-1, keepdims=True) + EPS)
            qn[0, h * BLK : (h + 1) * BLK, :] = (raw * inv * qg[...]).astype(bf16)
            qn[1, h * BLK : (h + 1) * BLK, :] = ds_[p, j, c, :, h * HD : (h + 1) * HD]

        q_pos = b * BLK + lax.broadcasted_iota(jnp.int32, (1, BLK), 1)
        q_first = firsts[b]

        def scores(t, carry):
            top, total = carry
            rows = cols(t * KT, KT)
            s = dot_nt(kn[p, rows, :], qn[0])
            k_pos = t * KT + lax.broadcasted_iota(jnp.int32, (KT, BLK), 0)
            allowed = (k_pos >= q_first) & (k_pos <= q_pos)
            s = jnp.concatenate(
                [jnp.where(allowed, s[:, h * BLK : (h + 1) * BLK], NEG) for h in range(4)], axis=1
            )
            new = jnp.maximum(top, jnp.max(fold(s, jnp.max), axis=0, keepdims=True))
            e = jnp.exp2((s - new) * (SCALE * LOG2E))
            es[rows, :] = e
            ms[t] = new
            total = total * jnp.exp2((top - new) * (SCALE * LOG2E)) + fold(e, jnp.sum)
            return new, total

        top, total = lax.fori_loop(
            0, n_tiles, scores, (jnp.full((1, CH), NEG, f32), jnp.zeros((8, CH), f32))
        )
        recip = 1.0 / jnp.sum(total, axis=0, keepdims=True)

        ot[...] = jnp.zeros_like(ot)

        def outs(t, carry):
            rows = cols(t * KT, KT)
            factor = jnp.exp2((ms[t] - top) * (SCALE * LOG2E)) * recip
            e = es[rows, :] * factor
            es[rows, :] = e
            pr = e.astype(bf16)
            ot[...] += dot_nn(vt_[p, :, rows], pr)
            dva[p, rows, :] += dot_nn(pr, qn[1])
            return carry

        lax.fori_loop(0, n_tiles, outs, 0)

        deltas = []
        for h in range(4):
            out = ot[:, h * BLK : (h + 1) * BLK].T.astype(bf16)
            os_[p, j, c, :, h * HD : (h + 1) * HD] = out
            up = qn[1, h * BLK : (h + 1) * BLK, :].astype(f32)
            deltas.append(jnp.sum((up * out.astype(f32)).T, axis=0, keepdims=True))
        delta = jnp.concatenate(deltas, axis=1)

        dqt[...] = jnp.zeros_like(dqt)

        def grads(t, carry):
            rows = cols(t * KT, KT)
            dp_ = dot_nt(vn[p, rows, :], qn[1])
            g = (es[rows, :] * (dp_ - delta) * SCALE).astype(bf16)
            dqt[...] += dot_nn(kt_[p, :, rows], g)
            dka[p, rows, :] += dot_nn(g, qn[0])
            return carry

        lax.fori_loop(0, n_tiles, grads, 0)

        for h in range(4):
            raw = qs[p, j, c, :, h * HD : (h + 1) * HD].astype(f32)
            inv = lax.rsqrt(jnp.mean(raw * raw, axis=-1, keepdims=True) + EPS)
            hat = raw * inv
            grad = dqt[:, h * BLK : (h + 1) * BLK].T
            gacc[0] += fold(grad * hat, jnp.sum)
            g = grad * qg[...]
            dqs[p, j, c, :, h * HD : (h + 1) * HD] = (
                inv * (g - hat * jnp.mean(g * hat, axis=-1, keepdims=True))
            ).astype(bf16)

        for i, (src, dst) in enumerate(((os_, o), (dqs, dq))):
            place = dst.at[:, cols(p * PART + me * OWN + c * CH, CH)]

            @pl.when(d == 0)
            def _():
                pltpu.make_async_copy(src.at[p, j, c], place, r_out.at[i, p, j, c]).start()

            @pl.when(d != 0)
            def _():
                remote(
                    src.at[p, j, c], place, s_out.at[i, p, d, c], r_out.at[i, p, me, c],
                    where(p, j),
                ).start()

        return carry

    lax.fori_loop(0, 16, unit, 0)

    def pack(t, carry):
        p, b = t // 16, t % 16
        rows = cols(b * BLK, BLK)
        sb[p, 0, b // SIDE, b % SIDE] = dka[p, rows, :].astype(bf16)
        sb[p, 1, b // SIDE, b % SIDE] = dva[p, rows, :].astype(bf16)
        return carry

    rs_sends = []
    for p in (0, 1):
        lax.fori_loop(p * 16, p * 16 + 16, pack, 0)
        other = mine[1 - p]
        for d in (1, 3, 2):
            j = (other + d) % SIDE
            src = sb.at[0, :, :, j] if p == 0 else sb.at[1, :, j]
            c = remote(
                src, rb.at[p, other], s_rs.at[p, d], r_rs.at[p, other], dev_of(1 - p, j)
            )
            c.start()
            rs_sends.append(c)

    f_sends = []
    for p in (0, 1):
        other = mine[1 - p]
        me = mine[p]
        for d in (1, 3, 2):
            blk = rb.at[p, (other + d) % SIDE]
            pltpu.make_async_copy(blk, blk, r_rs.at[p, (other + d) % SIDE]).wait()
        for dd in (1, 3, 2, 0):
            j = (me + dd) % SIDE
            b = j * SIDE + y if p == 0 else x * SIDE + j
            rows = cols(b * BLK, BLK)
            kgrad = dka[p, rows, :]
            vgrad = dva[p, rows, :]
            for d in (1, 2, 3):
                slot = (other + d) % SIDE
                kgrad = kgrad + rb[p, slot, 0, j].astype(f32)
                vgrad = vgrad + rb[p, slot, 1, j].astype(f32)
            raw = (kv[0, 0, j, y] if p == 0 else kv[1, 0, x, j]).astype(f32)
            inv = lax.rsqrt(jnp.mean(raw * raw, axis=-1, keepdims=True) + EPS)
            hat = raw * inv
            gacc[1] += fold(kgrad * hat, jnp.sum)
            g = kgrad * kg[...]
            fb[p, 0, j] = (inv * (g - hat * jnp.mean(g * hat, axis=-1, keepdims=True))).astype(
                bf16
            )
            fb[p, 1, j] = vgrad.astype(bf16)
            for i, dst in enumerate((dk, dv)):
                place = dst.at[:, cols(p * 512 + me * HD, HD)]
                if dd == 0:
                    pltpu.make_async_copy(fb.at[p, i, j], place, r_f.at[p, i, me]).start()
                else:
                    c = remote(
                        fb.at[p, i, j], place, s_f.at[p, i, dd], r_f.at[p, i, me], dev_of(p, j)
                    )
                    c.start()
                    f_sends.append(c)

    qgp[...] = jnp.sum(gacc[0], axis=0, keepdims=True)
    kgp[...] = jnp.sum(gacc[1], axis=0, keepdims=True)

    for c in kv_sends + ag_sends + in_sends + rs_sends + f_sends:
        c.wait_send()

    def drain(t, carry):
        i, p, d, c = t // 12, (t // 6) % 2, (t // 2) % 3 + 1, t % 2
        src = os_.at[0, 0, 0]
        pltpu.make_async_copy(src, src, s_out.at[i, p, d, c]).wait()
        return carry

    lax.fori_loop(0, 24, drain, 0)

    def arrive(t, carry):
        i, p, j, c = t // 16, (t // 8) % 2, (t // 2) % 4, t % 2
        place = o.at[:, cols(p * PART + j * OWN + c * CH, CH)]
        pltpu.make_async_copy(place, place, r_out.at[i, p, j, c]).wait()
        return carry

    lax.fori_loop(0, 32, arrive, 0)
    for p in (0, 1):
        for i, dst in enumerate((dk, dv)):
            for j in range(SIDE):
                place = dst.at[:, cols(p * 512 + j * HD, HD)]
                pltpu.make_async_copy(place, place, r_f.at[p, i, j]).wait()


def on_device(q_proj, k_proj, v_proj, q_gain, k_gain, dout, segments):
    rows = q_proj.shape[0]
    total_rows = rows * lax.axis_size("seq") * lax.axis_size("dp")
    ids = lax.dynamic_index_in_dim(
        segments.reshape(lax.axis_size("dp"), 16, BLK), lax.axis_index("dp"), 0, keepdims=False
    )
    any_ = pl.BlockSpec(memory_space=pl.ANY)
    vmem = pl.BlockSpec(memory_space=pltpu.VMEM)
    dma = pltpu.SemaphoreType.DMA
    length = SIDE * SIDE * BLK
    o, dq, dk, dv, qgp, kgp = pl.pallas_call(
        kernel,
        out_shape=(
            jax.ShapeDtypeStruct((rows, QH * HD), bf16),
            jax.ShapeDtypeStruct((rows, QH * HD), bf16),
            jax.ShapeDtypeStruct((rows, KVH * HD), bf16),
            jax.ShapeDtypeStruct((rows, KVH * HD), bf16),
            jax.ShapeDtypeStruct((1, HD), f32),
            jax.ShapeDtypeStruct((1, HD), f32),
        ),
        in_specs=[any_, any_, any_, any_, vmem, vmem, vmem],
        out_specs=(any_, any_, any_, any_, vmem, vmem),
        scratch_shapes=[
            pltpu.VMEM((2, SIDE, 2, BLK, CH), bf16),
            pltpu.VMEM((2, SIDE, 2, BLK, CH), bf16),
            pltpu.VMEM((2, 2, SIDE, SIDE, BLK, HD), bf16),
            pltpu.VMEM((2, length, HD), bf16),
            pltpu.VMEM((2, length, HD), bf16),
            pltpu.VMEM((2, HD, length), bf16),
            pltpu.VMEM((2, HD, length), bf16),
            pltpu.VMEM((2, SIDE, 2, BLK, CH), bf16),
            pltpu.VMEM((2, SIDE, 2, BLK, CH), bf16),
            pltpu.VMEM((length, CH), f32),
            pltpu.VMEM((8, 1, CH), f32),
            pltpu.VMEM((16, 1, BLK), jnp.int32),
            pltpu.VMEM((2, length, HD), f32),
            pltpu.VMEM((2, length, HD), f32),
            pltpu.VMEM((2, 2, SIDE, SIDE, BLK, HD), bf16),
            pltpu.VMEM((2, SIDE, 2, SIDE, BLK, HD), bf16),
            pltpu.VMEM((2, 2, SIDE, BLK, HD), bf16),
            pltpu.VMEM((2, CH, HD), bf16),
            pltpu.VMEM((HD, CH), f32),
            pltpu.VMEM((HD, CH), f32),
            pltpu.VMEM((2, 8, HD), f32),
            dma((2, 2, SIDE, 2)), dma((2, 2, SIDE, 2)),
            dma((2, 2, SIDE)), dma((2, 2, SIDE)),
            dma((2, SIDE)), dma((2, SIDE)),
            dma((2, 2, SIDE, 2)), dma((2, 2, SIDE, 2)),
            dma((2, SIDE)), dma((2, SIDE)),
            dma((2, 2, SIDE)), dma((2, 2, SIDE)),
        ],
        name="exchange_attend",
        cost_estimate=pl.CostEstimate(
            flops=20_000_000_000, bytes_accessed=20_000_000, transcendentals=10_000_000
        ),
        compiler_params=pltpu.CompilerParams(
            collective_id=0, has_side_effects=True, vmem_limit_bytes=48 << 20
        ),
    )(q_proj, k_proj, v_proj, dout, ids, q_gain.reshape(1, HD), k_gain.reshape(1, HD))
    sums = lax.psum(jnp.concatenate([qgp, kgp], axis=0), ("dp", "seq"))
    return (
        o,
        dq,
        dk,
        dv,
        sums[0] / math.sqrt(total_rows * QH),
        sums[1] / math.sqrt(total_rows * KVH),
    )


def solution(mesh):
    split = P(("dp", "seq"), None)
    return jax.shard_map(
        on_device,
        mesh=mesh,
        in_specs=(split, split, split, P(), P(), split, P()),
        out_specs=(split, split, split, split, P(), P()),
        check_vma=False,
    )
```

```python
import math

import jax
import jax.numpy as jnp
from jax import lax
from jax.experimental import pallas as pl
from jax.experimental.pallas import tpu as pltpu
from jax.sharding import PartitionSpec as P

QH = 64
KVH = 8
HD = 128
EPS = 1e-06
NEG = -1e30
MESH = pl.DeviceIdType.MESH
BLK = 128
ROWS = 8
SIDE = 4
PART = 4096
OWN = 1024
HEADS = 8
KT = 512
SCALE = 1.0 / math.sqrt(HD)
LOG2E = math.log2(math.e)
bf16 = jnp.bfloat16
f32 = jnp.float32


def dot_nt(a, b):
    return lax.dot_general(a, b, (((1,), (1,)), ((), ())), preferred_element_type=f32)


def dot_nn(a, b):
    return lax.dot_general(a, b, (((1,), (0,)), ((), ())), preferred_element_type=f32)


def fold(x, op):
    rows, cols = x.shape
    return op(x.reshape(rows // 8, 8, cols), axis=0)


def kernel(
    q, k, v, do, seg, qg, kg,
    o, dq, dk, dv, qgp, kgp,
    qs, ds_, kv, kn, vn, kt_, vt_, os_, dqs, es, ms, firsts, dka, dva, sb, rb, fb, qn, ot, dqt, gacc, gb,
    s_in, r_in, s_kv, r_kv, s_ag, r_ag, s_out, r_out, s_rs, r_rs, s_f, r_f, s_g, r_g,
):
    seq = lax.axis_index("seq")
    dp = lax.axis_index("dp")
    x, y = seq // SIDE, seq % SIDE
    mine = (x, y)

    def where(p, j):
        return (dp, lax.select(p == 0, j * SIDE + y, x * SIDE + j))

    def own(p):
        return lax.select(p == 0, x, y)

    def remote(src, dst, ss, rs, dev):
        return pltpu.make_async_remote_copy(
            src_ref=src, dst_ref=dst, send_sem=ss, recv_sem=rs, device_id=dev, device_id_type=MESH
        )

    def cols(start, width):
        return pl.ds(pl.multiple_of(start, width), width)

    def dev_of(p, j):
        return (dp, j * SIDE + y) if p == 0 else (dp, x * SIDE + j)

    barrier = pltpu.get_barrier_semaphore()
    for p in (0, 1):
        for d in (1, 2, 3):
            pl.semaphore_signal(
                barrier, inc=1, device_id=dev_of(p, (mine[p] + d) % SIDE), device_id_type=MESH
            )
    for d in range(1, ROWS):
        pl.semaphore_signal(
            barrier, inc=1, device_id=((dp + d) % ROWS, seq), device_id_type=MESH
        )

    for p in (0, 1):
        me = mine[p]
        for i, src in enumerate((k, v)):
            pltpu.make_async_copy(
                src.at[:, cols(p * 512 + me * HD, HD)], kv.at[p, i, x, y], r_kv.at[p, i, me]
            ).start()
    pl.semaphore_wait(barrier, 6 + ROWS - 1)

    kv_sends = []
    for d in (1, 3, 2):
        for p in (0, 1):
            me = mine[p]
            j = (me + d) % SIDE
            for i, src in enumerate((k, v)):
                c = remote(
                    src.at[:, cols(p * 512 + j * HD, HD)], kv.at[p, i, x, y],
                    s_kv.at[p, i, d], r_kv.at[p, i, me], dev_of(p, j),
                )
                c.start()
                kv_sends.append(c)

    for p in (0, 1):
        me = mine[p]
        for i, src in enumerate((q, do)):
            dst = (qs, ds_)[i]
            pltpu.make_async_copy(
                src.at[:, cols(p * PART + me * OWN, OWN)], dst.at[p, me], r_in.at[i, p, me]
            ).start()

    ag_sends = []
    for p in (0, 1):
        me = mine[p]
        other = mine[1 - p]
        for j in range(SIDE):
            for i in (0, 1):
                blk = kv.at[p, i, j, y] if p == 0 else kv.at[p, i, x, j]
                pltpu.make_async_copy(blk, blk, r_kv.at[p, i, j]).wait()
        held = kv.at[0, :, :, y] if p == 0 else kv.at[1, :, x]
        for d in (1, 3, 2):
            c = remote(
                held, held, s_ag.at[p, d], r_ag.at[p, other], dev_of(1 - p, (other + d) % SIDE)
            )
            c.start()
            ag_sends.append(c)

    in_sends = []
    for d in (1, 3, 2):
        for p in (0, 1):
            me = mine[p]
            j = (me + d) % SIDE
            for i, src in enumerate((q, do)):
                dst = (qs, ds_)[i]
                c = remote(
                    src.at[:, cols(p * PART + j * OWN, OWN)], dst.at[p, me],
                    s_in.at[i, p, d], r_in.at[i, p, me], dev_of(p, j),
                )
                c.start()
                in_sends.append(c)

    ids = seg[dp]
    first = jnp.zeros((16, BLK), jnp.int32)
    for value in range(7):
        hits = jnp.where(ids == value, 1, 0)
        count = jnp.sum(jnp.sum(hits, axis=1, keepdims=True), axis=0, keepdims=True)
        first = first + jnp.where(ids > value, count, 0)
    seg_first = first

    dka[...] = jnp.zeros_like(dka)
    dva[...] = jnp.zeros_like(dva)
    gacc[...] = jnp.zeros_like(gacc)
    for i in range(16):
        firsts[i] = seg_first[i : i + 1, :]

    for p in (0, 1):
        other = mine[1 - p]
        for d in (1, 3, 2):
            j = (other + d) % SIDE
            blk = kv.at[0, :, :, j] if p == 0 else kv.at[1, :, j]
            pltpu.make_async_copy(blk, blk, r_ag.at[p, j]).wait()

    def prep(t, carry):
        p, b = t // 16, t % 16
        raw = kv[p, 0, b // SIDE, b % SIDE].astype(f32)
        inv = lax.rsqrt(jnp.mean(raw * raw, axis=-1, keepdims=True) + EPS)
        normed = (raw * inv * kg[...]).astype(bf16)
        rows = cols(b * BLK, BLK)
        kn[p, rows, :] = normed
        kt_[p, :, rows] = normed.astype(f32).T.astype(bf16)
        val = kv[p, 1, b // SIDE, b % SIDE]
        vn[p, rows, :] = val
        vt_[p, :, rows] = val.astype(f32).T.astype(bf16)
        return carry

    lax.fori_loop(0, 32, prep, 0)

    def unit(u, carry):
        p = u % 2
        step = u // 2
        d = lax.select(step == 2, 3, lax.select(step == 3, 2, step))
        me = own(p)
        j = (me + d) % SIDE
        b = lax.select(p == 0, j * SIDE + y, x * SIDE + j)
        n_tiles = b // (KT // BLK) + 1
        for i, dst in enumerate((qs, ds_)):
            blk = dst.at[p, j]
            pltpu.make_async_copy(blk, blk, r_in.at[i, p, j]).wait()

        for h in range(HEADS):
            raw = qs[p, j, :, h * HD : (h + 1) * HD].astype(f32)
            inv = lax.rsqrt(jnp.mean(raw * raw, axis=-1, keepdims=True) + EPS)
            qn[0, h * BLK : (h + 1) * BLK, :] = (raw * inv * qg[...]).astype(bf16)
            qn[1, h * BLK : (h + 1) * BLK, :] = ds_[p, j, :, h * HD : (h + 1) * HD]

        q_pos = b * BLK + lax.broadcasted_iota(jnp.int32, (1, BLK), 1)
        q_first = firsts[b]

        def scores(t, carry):
            top, total = carry
            rows = cols(t * KT, KT)
            s = dot_nt(kn[p, rows, :], qn[0])
            k_pos = t * KT + lax.broadcasted_iota(jnp.int32, (KT, BLK), 0)
            allowed = (k_pos >= q_first) & (k_pos <= q_pos)
            s = jnp.concatenate(
                [jnp.where(allowed, s[:, h * BLK : (h + 1) * BLK], NEG) for h in range(HEADS)], axis=1
            )
            new = jnp.maximum(top, jnp.max(fold(s, jnp.max), axis=0, keepdims=True))
            e = jnp.exp2((s - new) * (SCALE * LOG2E))
            es[rows, :] = e
            ms[t] = new
            total = total * jnp.exp2((top - new) * (SCALE * LOG2E)) + fold(e, jnp.sum)
            return new, total

        top, total = lax.fori_loop(
            0, n_tiles, scores, (jnp.full((1, OWN), NEG, f32), jnp.zeros((8, OWN), f32))
        )
        recip = 1.0 / jnp.sum(total, axis=0, keepdims=True)

        ot[...] = jnp.zeros_like(ot)

        def outs(t, carry):
            rows = cols(t * KT, KT)
            factor = jnp.exp2((ms[t] - top) * (SCALE * LOG2E)) * recip
            pr = (es[rows, :] * factor).astype(bf16)
            ot[...] += dot_nn(vt_[p, :, rows], pr)
            dva[p, rows, :] += dot_nn(pr, qn[1])
            return carry

        lax.fori_loop(0, n_tiles, outs, 0)

        deltas = []
        for h in range(HEADS):
            out = ot[:, h * BLK : (h + 1) * BLK].T.astype(bf16)
            os_[p, j, :, h * HD : (h + 1) * HD] = out
            up = qn[1, h * BLK : (h + 1) * BLK, :].astype(f32)
            deltas.append(jnp.sum((up * out.astype(f32)).T, axis=0, keepdims=True))
        delta = jnp.concatenate(deltas, axis=1)

        dqt[...] = jnp.zeros_like(dqt)

        def grads(t, carry):
            rows = cols(t * KT, KT)
            dp_ = dot_nt(vn[p, rows, :], qn[1])
            factor = jnp.exp2((ms[t] - top) * (SCALE * LOG2E)) * (recip * SCALE)
            g = ((es[rows, :] * factor) * (dp_ - delta)).astype(bf16)
            dqt[...] += dot_nn(kt_[p, :, rows], g)
            dka[p, rows, :] += dot_nn(g, qn[0])
            return carry

        lax.fori_loop(0, n_tiles, grads, 0)

        for h in range(HEADS):
            raw = qs[p, j, :, h * HD : (h + 1) * HD].astype(f32)
            inv = lax.rsqrt(jnp.mean(raw * raw, axis=-1, keepdims=True) + EPS)
            hat = raw * inv
            grad = dqt[:, h * BLK : (h + 1) * BLK].T
            gacc[0] += fold(grad * hat, jnp.sum)
            g = grad * qg[...]
            dqs[p, j, :, h * HD : (h + 1) * HD] = (
                inv * (g - hat * jnp.mean(g * hat, axis=-1, keepdims=True))
            ).astype(bf16)

        for i, (src, dst) in enumerate(((os_, o), (dqs, dq))):
            place = dst.at[:, cols(p * PART + me * OWN, OWN)]

            @pl.when(d == 0)
            def _():
                pltpu.make_async_copy(src.at[p, j], place, r_out.at[i, p, j]).start()

            @pl.when(d != 0)
            def _():
                remote(
                    src.at[p, j], place, s_out.at[i, p, d], r_out.at[i, p, me],
                    where(p, j),
                ).start()

        return carry

    lax.fori_loop(0, 8, unit, 0)

    def pack(t, carry):
        p, b = t // 16, t % 16
        rows = cols(b * BLK, BLK)
        sb[p, 0, b // SIDE, b % SIDE] = dka[p, rows, :].astype(bf16)
        sb[p, 1, b // SIDE, b % SIDE] = dva[p, rows, :].astype(bf16)
        return carry

    rs_sends = []
    for p in (0, 1):
        lax.fori_loop(p * 16, p * 16 + 16, pack, 0)
        other = mine[1 - p]
        for d in (1, 3, 2):
            j = (other + d) % SIDE
            src = sb.at[0, :, :, j] if p == 0 else sb.at[1, :, j]
            c = remote(
                src, rb.at[p, other], s_rs.at[p, d], r_rs.at[p, other], dev_of(1 - p, j)
            )
            c.start()
            rs_sends.append(c)

    f_sends = []
    for p in (0, 1):
        other = mine[1 - p]
        me = mine[p]
        for d in (1, 3, 2):
            blk = rb.at[p, (other + d) % SIDE]
            pltpu.make_async_copy(blk, blk, r_rs.at[p, (other + d) % SIDE]).wait()
        for dd in (1, 3, 2, 0):
            j = (me + dd) % SIDE
            b = j * SIDE + y if p == 0 else x * SIDE + j
            rows = cols(b * BLK, BLK)
            kgrad = dka[p, rows, :]
            vgrad = dva[p, rows, :]
            for d in (1, 2, 3):
                slot = (other + d) % SIDE
                kgrad = kgrad + rb[p, slot, 0, j].astype(f32)
                vgrad = vgrad + rb[p, slot, 1, j].astype(f32)
            raw = (kv[0, 0, j, y] if p == 0 else kv[1, 0, x, j]).astype(f32)
            inv = lax.rsqrt(jnp.mean(raw * raw, axis=-1, keepdims=True) + EPS)
            hat = raw * inv
            gacc[1] += fold(kgrad * hat, jnp.sum)
            g = kgrad * kg[...]
            fb[p, 0, j] = (inv * (g - hat * jnp.mean(g * hat, axis=-1, keepdims=True))).astype(
                bf16
            )
            fb[p, 1, j] = vgrad.astype(bf16)
            for i, dst in enumerate((dk, dv)):
                place = dst.at[:, cols(p * 512 + me * HD, HD)]
                if dd == 0:
                    pltpu.make_async_copy(fb.at[p, i, j], place, r_f.at[p, i, me]).start()
                else:
                    c = remote(
                        fb.at[p, i, j], place, s_f.at[p, i, dd], r_f.at[p, i, me], dev_of(p, j)
                    )
                    c.start()
                    f_sends.append(c)

    held = jnp.concatenate(
        [jnp.sum(gacc[i], axis=0, keepdims=True) for i in (0, 1)] + [jnp.zeros((6, HD), f32)],
        axis=0,
    )
    g_sends = []
    for n, (place, count) in enumerate(((x, SIDE), (y, SIDE), (dp, ROWS))):
        gb[n, place] = held
        for d in range(1, count):
            j = (place + d) % count
            dev = dev_of(n, j) if n < 2 else (j, seq)
            c = remote(gb.at[n, place], gb.at[n, place], s_g.at[n, d], r_g.at[n, place], dev)
            c.start()
            g_sends.append(c)
        for d in range(1, count):
            blk = gb.at[n, (place + d) % count]
            pltpu.make_async_copy(blk, blk, r_g.at[n, (place + d) % count]).wait()
        held = gb[n, 0]
        for j in range(1, count):
            held = held + gb[n, j]
    tokens = ROWS * SIDE * SIDE * BLK
    qgp[...] = held[0:1] / math.sqrt(tokens * QH)
    kgp[...] = held[1:2] / math.sqrt(tokens * KVH)

    for c in kv_sends + ag_sends + in_sends + rs_sends + f_sends + g_sends:
        c.wait_send()

    def drain(t, carry):
        i, p, d = t // 6, (t // 3) % 2, t % 3 + 1
        src = os_.at[0, 0]
        pltpu.make_async_copy(src, src, s_out.at[i, p, d]).wait()
        return carry

    lax.fori_loop(0, 12, drain, 0)

    def arrive(t, carry):
        i, p, j = t // 8, (t // 4) % 2, t % 4
        place = o.at[:, cols(p * PART + j * OWN, OWN)]
        pltpu.make_async_copy(place, place, r_out.at[i, p, j]).wait()
        return carry

    lax.fori_loop(0, 16, arrive, 0)
    for p in (0, 1):
        for i, dst in enumerate((dk, dv)):
            for j in range(SIDE):
                place = dst.at[:, cols(p * 512 + j * HD, HD)]
                pltpu.make_async_copy(place, place, r_f.at[p, i, j]).wait()


def on_device(q_proj, k_proj, v_proj, q_gain, k_gain, dout, segments):
    rows = q_proj.shape[0]
    ids = segments.reshape(ROWS, SIDE * SIDE, BLK)
    any_ = pl.BlockSpec(memory_space=pl.ANY)
    vmem = pl.BlockSpec(memory_space=pltpu.VMEM)
    dma = pltpu.SemaphoreType.DMA
    length = SIDE * SIDE * BLK
    o, dq, dk, dv, qgp, kgp = pl.pallas_call(
        kernel,
        out_shape=(
            jax.ShapeDtypeStruct((rows, QH * HD), bf16),
            jax.ShapeDtypeStruct((rows, QH * HD), bf16),
            jax.ShapeDtypeStruct((rows, KVH * HD), bf16),
            jax.ShapeDtypeStruct((rows, KVH * HD), bf16),
            jax.ShapeDtypeStruct((1, HD), f32),
            jax.ShapeDtypeStruct((1, HD), f32),
        ),
        in_specs=[any_, any_, any_, any_, vmem, vmem, vmem],
        out_specs=(any_, any_, any_, any_, vmem, vmem),
        scratch_shapes=[
            pltpu.VMEM((2, SIDE, BLK, OWN), bf16),
            pltpu.VMEM((2, SIDE, BLK, OWN), bf16),
            pltpu.VMEM((2, 2, SIDE, SIDE, BLK, HD), bf16),
            pltpu.VMEM((2, length, HD), bf16),
            pltpu.VMEM((2, length, HD), bf16),
            pltpu.VMEM((2, HD, length), bf16),
            pltpu.VMEM((2, HD, length), bf16),
            pltpu.VMEM((2, SIDE, BLK, OWN), bf16),
            pltpu.VMEM((2, SIDE, BLK, OWN), bf16),
            pltpu.VMEM((length, OWN), f32),
            pltpu.VMEM((SIDE, 1, OWN), f32),
            pltpu.VMEM((16, 1, BLK), jnp.int32),
            pltpu.VMEM((2, length, HD), f32),
            pltpu.VMEM((2, length, HD), f32),
            pltpu.VMEM((2, 2, SIDE, SIDE, BLK, HD), bf16),
            pltpu.VMEM((2, SIDE, 2, SIDE, BLK, HD), bf16),
            pltpu.VMEM((2, 2, SIDE, BLK, HD), bf16),
            pltpu.VMEM((2, OWN, HD), bf16),
            pltpu.VMEM((HD, OWN), f32),
            pltpu.VMEM((HD, OWN), f32),
            pltpu.VMEM((2, 8, HD), f32),
            pltpu.VMEM((3, ROWS, 8, HD), f32),
            dma((2, 2, SIDE)), dma((2, 2, SIDE)),
            dma((2, 2, SIDE)), dma((2, 2, SIDE)),
            dma((2, SIDE)), dma((2, SIDE)),
            dma((2, 2, SIDE)), dma((2, 2, SIDE)),
            dma((2, SIDE)), dma((2, SIDE)),
            dma((2, 2, SIDE)), dma((2, 2, SIDE)),
            dma((3, ROWS)), dma((3, ROWS)),
        ],
        name="exchange_attend",
        cost_estimate=pl.CostEstimate(
            flops=20_000_000_000, bytes_accessed=20_000_000, transcendentals=10_000_000
        ),
        compiler_params=pltpu.CompilerParams(
            collective_id=0, has_side_effects=True, vmem_limit_bytes=58 << 20
        ),
    )(q_proj, k_proj, v_proj, dout, ids, q_gain.reshape(1, HD), k_gain.reshape(1, HD))
    return o, dq, dk, dv, qgp.reshape(HD), kgp.reshape(HD)


def solution(mesh):
    split = P(("dp", "seq"), None)
    return jax.shard_map(
        on_device,
        mesh=mesh,
        in_specs=(split, split, split, P(), P(), split, P()),
        out_specs=(split, split, split, split, P(), P()),
        check_vma=False,
    )
```

```python
import functools
import math

import jax
import jax.numpy as jnp
from jax import lax
from jax.experimental import pallas as pl
from jax.experimental.pallas import tpu as pltpu
from jax.sharding import PartitionSpec as P

QH = 64
KVH = 8
HD = 128
EPS = 1e-06
NEG = -1e30
MESH = pl.DeviceIdType.MESH
BLK = 128
ROWS = 8
SIDE = 4
PART = 4096
OWN = 1024
HEADS = 8
KT = 512
EARLY = (1,)
SCALE = 1.0 / math.sqrt(HD)
LOG2E = math.log2(math.e)
bf16 = jnp.bfloat16
f32 = jnp.float32


def dot_nt(a, b):
    return lax.dot_general(a, b, (((1,), (1,)), ((), ())), preferred_element_type=f32)


def dot_nn(a, b):
    return lax.dot_general(a, b, (((1,), (0,)), ((), ())), preferred_element_type=f32)


def fold(x, op):
    rows, cols = x.shape
    return op(x.reshape(rows // 8, 8, cols), axis=0)


def kernel(
    q, k, v, do, seg, qg, kg,
    o, dq, dk, dv, qgp, kgp,
    qs, ds_, kv, kn, vn, kt_, vt_, os_, dqs, es, ms, firsts, dka, dva, sb, rb, fb, qn, ot, dqt, gacc, gb,
    s_in, r_in, s_kv, r_kv, s_ag, r_ag, s_out, r_out, s_rs, r_rs, s_f, r_f, s_g, r_g,
):
    seq = lax.axis_index("seq")
    dp = lax.axis_index("dp")
    x, y = seq // SIDE, seq % SIDE
    mine = (x, y)

    def own(p):
        return lax.select(p == 0, x, y)

    def remote(src, dst, ss, rs, dev):
        return pltpu.make_async_remote_copy(
            src_ref=src, dst_ref=dst, send_sem=ss, recv_sem=rs, device_id=dev, device_id_type=MESH
        )

    def cols(start, width):
        return pl.ds(pl.multiple_of(start, width), width)

    def dev_of(p, j):
        return (dp, j * SIDE + y) if p == 0 else (dp, x * SIDE + j)

    barrier = pltpu.get_barrier_semaphore()
    for p in (0, 1):
        for d in (1, 2, 3):
            pl.semaphore_signal(
                barrier, inc=1, device_id=dev_of(p, (mine[p] + d) % SIDE), device_id_type=MESH
            )
    for d in range(1, ROWS):
        pl.semaphore_signal(
            barrier, inc=1, device_id=((dp + d) % ROWS, seq), device_id_type=MESH
        )

    for p in (0, 1):
        me = mine[p]
        for i, src in enumerate((k, v)):
            pltpu.make_async_copy(
                src.at[:, cols(p * 512 + me * HD, HD)], kv.at[p, i, x, y], r_kv.at[p, i, me]
            ).start()
    pl.semaphore_wait(barrier, 6 + ROWS - 1)

    kv_sends = []
    for i, src in enumerate((k, v)):
        for d in (1, 3, 2):
            for p in (0, 1):
                me = mine[p]
                j = (me + d) % SIDE
                c = remote(
                    src.at[:, cols(p * 512 + j * HD, HD)], kv.at[p, i, x, y],
                    s_kv.at[p, i, d], r_kv.at[p, i, me], dev_of(p, j),
                )
                c.start()
                kv_sends.append(c)

    for p in (0, 1):
        me = mine[p]
        for i, src in enumerate((q, do)):
            dst = (qs, ds_)[i]
            pltpu.make_async_copy(
                src.at[:, cols(p * PART + me * OWN, OWN)], dst.at[p, me], r_in.at[i, p, me]
            ).start()

    ag_sends = []
    for i in (0, 1):
        for p in (0, 1):
            other = mine[1 - p]
            for j in range(SIDE):
                blk = kv.at[p, i, j, y] if p == 0 else kv.at[p, i, x, j]
                pltpu.make_async_copy(blk, blk, r_kv.at[p, i, j]).wait()
            held = kv.at[0, i, :, y] if p == 0 else kv.at[1, i, x]
            for d in (1, 3, 2):
                c = remote(
                    held, held, s_ag.at[p, i, d], r_ag.at[p, i, other],
                    dev_of(1 - p, (other + d) % SIDE),
                )
                c.start()
                ag_sends.append(c)

    in_sends = []

    def send_in(d):
        for p in (0, 1):
            me = mine[p]
            j = (me + d) % SIDE
            for i, src in enumerate((q, do)):
                dst = (qs, ds_)[i]
                c = remote(
                    src.at[:, cols(p * PART + j * OWN, OWN)], dst.at[p, me],
                    s_in.at[i, p, d], r_in.at[i, p, me], dev_of(p, j),
                )
                c.start()
                in_sends.append(c)

    for d in EARLY:
        send_in(d)

    ids = seg[dp]
    first = jnp.zeros((16, BLK), jnp.int32)
    for value in range(7):
        hits = jnp.where(ids == value, 1, 0)
        count = jnp.sum(jnp.sum(hits, axis=1, keepdims=True), axis=0, keepdims=True)
        first = first + jnp.where(ids > value, count, 0)
    seg_first = first

    dka[...] = jnp.zeros_like(dka)
    dva[...] = jnp.zeros_like(dva)
    gacc[...] = jnp.zeros_like(gacc)
    for i in range(16):
        firsts[i] = seg_first[i : i + 1, :]

    def prep(p, i, place):
        def block(n, carry):
            xb, yb = (n, place) if p == 0 else (place, n)
            rows = cols((xb * SIDE + yb) * BLK, BLK)
            if i == 0:
                raw = kv[p, 0, xb, yb].astype(f32)
                inv = lax.rsqrt(jnp.mean(raw * raw, axis=-1, keepdims=True) + EPS)
                normed = (raw * inv * kg[...]).astype(bf16)
                kn[p, rows, :] = normed
                kt_[p, :, rows] = normed.astype(f32).T.astype(bf16)
            else:
                val = kv[p, 1, xb, yb]
                vn[p, rows, :] = val
                vt_[p, :, rows] = val.astype(f32).T.astype(bf16)
            return carry

        lax.fori_loop(0, SIDE, block, 0)

    def gathered(i):
        for p in (0, 1):
            prep(p, i, mine[1 - p])
        for d in (1, 3, 2):
            for p in (0, 1):
                j = (mine[1 - p] + d) % SIDE
                blk = kv.at[0, i, :, j] if p == 0 else kv.at[1, i, j]
                pltpu.make_async_copy(blk, blk, r_ag.at[p, i, j]).wait()
                prep(p, i, j)

    gathered(0)
    for d in (1, 3, 2):
        if d not in EARLY:
            send_in(d)

    def share(p, i):
        acc = (dka, dva)[i]

        def pack(b, carry):
            sb[p, i, b // SIDE, b % SIDE] = acc[p, cols(b * BLK, BLK), :].astype(bf16)
            return carry

        lax.fori_loop(0, SIDE * SIDE, pack, 0)
        other = mine[1 - p]
        for d in (1, 3, 2):
            j = (other + d) % SIDE
            src = sb.at[0, i, :, j] if p == 0 else sb.at[1, i, j]
            remote(
                src, rb.at[p, other, i], s_rs.at[p, i, d], r_rs.at[p, i, other], dev_of(1 - p, j)
            ).start()

    last_of = (6, 7)

    def unit(u, carry):
        p = u % 2
        step = u // 2
        d = lax.select(step == 2, 3, lax.select(step == 3, 2, step))
        me = own(p)
        j = (me + d) % SIDE
        b = lax.select(p == 0, j * SIDE + y, x * SIDE + j)
        n_tiles = b // (KT // BLK) + 1
        for i, dst in enumerate((qs, ds_)):
            blk = dst.at[p, j]
            pltpu.make_async_copy(blk, blk, r_in.at[i, p, j]).wait()

        for h in range(HEADS):
            raw = qs[p, j, :, h * HD : (h + 1) * HD].astype(f32)
            inv = lax.rsqrt(jnp.mean(raw * raw, axis=-1, keepdims=True) + EPS)
            qn[0, h * BLK : (h + 1) * BLK, :] = (raw * inv * qg[...]).astype(bf16)
            qn[1, h * BLK : (h + 1) * BLK, :] = ds_[p, j, :, h * HD : (h + 1) * HD]

        q_pos = b * BLK + lax.broadcasted_iota(jnp.int32, (1, BLK), 1)
        q_first = firsts[b]

        def scores(t, carry):
            top, total = carry
            rows = cols(t * KT, KT)
            s = dot_nt(kn[p, rows, :], qn[0])
            k_pos = t * KT + lax.broadcasted_iota(jnp.int32, (KT, BLK), 0)
            allowed = (k_pos >= q_first) & (k_pos <= q_pos)
            s = jnp.concatenate(
                [jnp.where(allowed, s[:, h * BLK : (h + 1) * BLK], NEG) for h in range(HEADS)], axis=1
            )
            new = jnp.maximum(top, jnp.max(fold(s, jnp.max), axis=0, keepdims=True))
            e = jnp.exp2((s - new) * (SCALE * LOG2E))
            es[rows, :] = e
            ms[t] = new
            total = total * jnp.exp2((top - new) * (SCALE * LOG2E)) + fold(e, jnp.sum)
            return new, total

        top, total = lax.fori_loop(
            0, n_tiles, scores, (jnp.full((1, OWN), NEG, f32), jnp.zeros((8, OWN), f32))
        )
        recip = 1.0 / jnp.sum(total, axis=0, keepdims=True)
        pl.when(u == 0)(functools.partial(gathered, 1))

        ot[...] = jnp.zeros_like(ot)

        def outs(t, carry):
            rows = cols(t * KT, KT)
            factor = jnp.exp2((ms[t] - top) * (SCALE * LOG2E)) * recip
            pr = (es[rows, :] * factor).astype(bf16)
            ot[...] += dot_nn(vt_[p, :, rows], pr)
            dva[p, rows, :] += dot_nn(pr, qn[1])
            return carry

        lax.fori_loop(0, n_tiles, outs, 0)
        for part in (0, 1):
            pl.when(u == last_of[part])(functools.partial(share, part, 1))

        def send_out(i, src, dst):
            place = dst.at[:, cols(p * PART + me * OWN, OWN)]

            @pl.when(d == 0)
            def _():
                pltpu.make_async_copy(src.at[p, j], place, r_out.at[i, p, j]).start()

            @pl.when(d != 0)
            def _():
                remote(
                    src.at[p, j], place, s_out.at[i, p, d], r_out.at[i, p, me], (dp, b)
                ).start()

        deltas = []
        for h in range(HEADS):
            out = ot[:, h * BLK : (h + 1) * BLK].T.astype(bf16)
            os_[p, j, :, h * HD : (h + 1) * HD] = out
            up = qn[1, h * BLK : (h + 1) * BLK, :].astype(f32)
            deltas.append(jnp.sum((up * out.astype(f32)).T, axis=0, keepdims=True))
        delta = jnp.concatenate(deltas, axis=1)
        send_out(0, os_, o)

        dqt[...] = jnp.zeros_like(dqt)

        def grads(t, carry):
            rows = cols(t * KT, KT)
            dp_ = dot_nt(vn[p, rows, :], qn[1])
            factor = jnp.exp2((ms[t] - top) * (SCALE * LOG2E)) * (recip * SCALE)
            g = ((es[rows, :] * factor) * (dp_ - delta)).astype(bf16)
            dqt[...] += dot_nn(kt_[p, :, rows], g)
            dka[p, rows, :] += dot_nn(g, qn[0])
            return carry

        lax.fori_loop(0, n_tiles, grads, 0)
        for part in (0, 1):
            pl.when(u == last_of[part])(functools.partial(share, part, 0))

        for h in range(HEADS):
            raw = qs[p, j, :, h * HD : (h + 1) * HD].astype(f32)
            inv = lax.rsqrt(jnp.mean(raw * raw, axis=-1, keepdims=True) + EPS)
            hat = raw * inv
            grad = dqt[:, h * BLK : (h + 1) * BLK].T
            gacc[0] += fold(grad * hat, jnp.sum)
            g = grad * qg[...]
            dqs[p, j, :, h * HD : (h + 1) * HD] = (
                inv * (g - hat * jnp.mean(g * hat, axis=-1, keepdims=True))
            ).astype(bf16)

        send_out(1, dqs, dq)

        return carry

    lax.fori_loop(0, 8, unit, 0)

    def key_gain(t, carry):
        p, b = t // 16, t % 16
        raw = kv[p, 0, b // SIDE, b % SIDE].astype(f32)
        inv = lax.rsqrt(jnp.mean(raw * raw, axis=-1, keepdims=True) + EPS)
        gacc[1] += fold(dka[p, cols(b * BLK, BLK), :] * (raw * inv), jnp.sum)
        return carry

    lax.fori_loop(0, 32, key_gain, 0)

    g_sends = []
    stages = ((dp, ROWS), (x, SIDE), (y, SIDE))

    def gain_send(n, held):
        place, count = stages[n]
        gb[n, place] = held
        for d in range(1, count):
            j = (place + d) % count
            dev = (j, seq) if n == 0 else dev_of(n - 1, j)
            c = remote(gb.at[n, place], gb.at[n, place], s_g.at[n, d], r_g.at[n, place], dev)
            c.start()
            g_sends.append(c)

    def gain_sum(n):
        place, count = stages[n]
        for d in range(1, count):
            blk = gb.at[n, (place + d) % count]
            pltpu.make_async_copy(blk, blk, r_g.at[n, (place + d) % count]).wait()
        held = gb[n, 0]
        for j in range(1, count):
            held = held + gb[n, j]
        return held

    gain_send(
        0,
        jnp.concatenate(
            [jnp.sum(gacc[i], axis=0, keepdims=True) for i in (0, 1)]
            + [jnp.zeros((6, HD), f32)],
            axis=0,
        ),
    )
    gain_send(1, gain_sum(0))

    f_sends = []
    for p in (0, 1):
        other = mine[1 - p]
        me = mine[p]
        for d in (1, 3, 2):
            slot = (other + d) % SIDE
            for i in (0, 1):
                blk = rb.at[p, slot, i]
                pltpu.make_async_copy(blk, blk, r_rs.at[p, i, slot]).wait()
        for dd in (1, 3, 2, 0):
            j = (me + dd) % SIDE
            b = j * SIDE + y if p == 0 else x * SIDE + j
            rows = cols(b * BLK, BLK)
            kgrad = dka[p, rows, :]
            vgrad = dva[p, rows, :]
            for d in (1, 2, 3):
                slot = (other + d) % SIDE
                kgrad = kgrad + rb[p, slot, 0, j].astype(f32)
                vgrad = vgrad + rb[p, slot, 1, j].astype(f32)
            raw = (kv[0, 0, j, y] if p == 0 else kv[1, 0, x, j]).astype(f32)
            inv = lax.rsqrt(jnp.mean(raw * raw, axis=-1, keepdims=True) + EPS)
            hat = raw * inv
            g = kgrad * kg[...]
            fb[p, 0, j] = (inv * (g - hat * jnp.mean(g * hat, axis=-1, keepdims=True))).astype(
                bf16
            )
            fb[p, 1, j] = vgrad.astype(bf16)
            for i, dst in enumerate((dk, dv)):
                place = dst.at[:, cols(p * 512 + me * HD, HD)]
                if dd == 0:
                    pltpu.make_async_copy(fb.at[p, i, j], place, r_f.at[p, i, me]).start()
                else:
                    c = remote(
                        fb.at[p, i, j], place, s_f.at[p, i, dd], r_f.at[p, i, me], dev_of(p, j)
                    )
                    c.start()
                    f_sends.append(c)

    gain_send(2, gain_sum(1))
    held = gain_sum(2)
    tokens = ROWS * SIDE * SIDE * BLK
    qgp[...] = held[0:1] / math.sqrt(tokens * QH)
    kgp[...] = held[1:2] / math.sqrt(tokens * KVH)

    for c in kv_sends + ag_sends + in_sends + f_sends + g_sends:
        c.wait_send()

    def drain(t, carry):
        i, p, d = t // 6, (t // 3) % 2, t % 3 + 1
        src = os_.at[0, 0]
        pltpu.make_async_copy(src, src, s_out.at[i, p, d]).wait()
        return carry

    lax.fori_loop(0, 12, drain, 0)

    for p in (0, 1):
        for i in (0, 1):
            for d in (1, 2, 3):
                blk = rb.at[0, 0, 0]
                pltpu.make_async_copy(blk, blk, s_rs.at[p, i, d]).wait()

    def arrive(t, carry):
        i, p, j = t // 8, (t // 4) % 2, t % 4
        place = o.at[:, cols(p * PART + j * OWN, OWN)]
        pltpu.make_async_copy(place, place, r_out.at[i, p, j]).wait()
        return carry

    lax.fori_loop(0, 16, arrive, 0)
    for p in (0, 1):
        for i, dst in enumerate((dk, dv)):
            for j in range(SIDE):
                place = dst.at[:, cols(p * 512 + j * HD, HD)]
                pltpu.make_async_copy(place, place, r_f.at[p, i, j]).wait()


def on_device(q_proj, k_proj, v_proj, q_gain, k_gain, dout, segments):
    rows = q_proj.shape[0]
    ids = segments.reshape(ROWS, SIDE * SIDE, BLK)
    any_ = pl.BlockSpec(memory_space=pl.ANY)
    vmem = pl.BlockSpec(memory_space=pltpu.VMEM)
    dma = pltpu.SemaphoreType.DMA
    length = SIDE * SIDE * BLK
    o, dq, dk, dv, qgp, kgp = pl.pallas_call(
        kernel,
        out_shape=(
            jax.ShapeDtypeStruct((rows, QH * HD), bf16),
            jax.ShapeDtypeStruct((rows, QH * HD), bf16),
            jax.ShapeDtypeStruct((rows, KVH * HD), bf16),
            jax.ShapeDtypeStruct((rows, KVH * HD), bf16),
            jax.ShapeDtypeStruct((1, HD), f32),
            jax.ShapeDtypeStruct((1, HD), f32),
        ),
        in_specs=[any_, any_, any_, any_, vmem, vmem, vmem],
        out_specs=(any_, any_, any_, any_, vmem, vmem),
        scratch_shapes=[
            pltpu.VMEM((2, SIDE, BLK, OWN), bf16),
            pltpu.VMEM((2, SIDE, BLK, OWN), bf16),
            pltpu.VMEM((2, 2, SIDE, SIDE, BLK, HD), bf16),
            pltpu.VMEM((2, length, HD), bf16),
            pltpu.VMEM((2, length, HD), bf16),
            pltpu.VMEM((2, HD, length), bf16),
            pltpu.VMEM((2, HD, length), bf16),
            pltpu.VMEM((2, SIDE, BLK, OWN), bf16),
            pltpu.VMEM((2, SIDE, BLK, OWN), bf16),
            pltpu.VMEM((length, OWN), f32),
            pltpu.VMEM((SIDE, 1, OWN), f32),
            pltpu.VMEM((16, 1, BLK), jnp.int32),
            pltpu.VMEM((2, length, HD), f32),
            pltpu.VMEM((2, length, HD), f32),
            pltpu.VMEM((2, 2, SIDE, SIDE, BLK, HD), bf16),
            pltpu.VMEM((2, SIDE, 2, SIDE, BLK, HD), bf16),
            pltpu.VMEM((2, 2, SIDE, BLK, HD), bf16),
            pltpu.VMEM((2, OWN, HD), bf16),
            pltpu.VMEM((HD, OWN), f32),
            pltpu.VMEM((HD, OWN), f32),
            pltpu.VMEM((2, 8, HD), f32),
            pltpu.VMEM((3, ROWS, 8, HD), f32),
            dma((2, 2, SIDE)), dma((2, 2, SIDE)),
            dma((2, 2, SIDE)), dma((2, 2, SIDE)),
            dma((2, 2, SIDE)), dma((2, 2, SIDE)),
            dma((2, 2, SIDE)), dma((2, 2, SIDE)),
            dma((2, 2, SIDE)), dma((2, 2, SIDE)),
            dma((2, 2, SIDE)), dma((2, 2, SIDE)),
            dma((3, ROWS)), dma((3, ROWS)),
        ],
        name="exchange_attend",
        cost_estimate=pl.CostEstimate(
            flops=20_000_000_000, bytes_accessed=20_000_000, transcendentals=10_000_000
        ),
        compiler_params=pltpu.CompilerParams(
            collective_id=0, has_side_effects=True, vmem_limit_bytes=58 << 20
        ),
    )(q_proj, k_proj, v_proj, dout, ids, q_gain.reshape(1, HD), k_gain.reshape(1, HD))
    return o, dq, dk, dv, qgp.reshape(HD), kgp.reshape(HD)


def solution(mesh):
    split = P(("dp", "seq"), None)
    return jax.shard_map(
        on_device,
        mesh=mesh,
        in_specs=(split, split, split, P(), P(), split, P()),
        out_specs=(split, split, split, split, P(), P()),
        check_vma=False,
    )
```

```python
import functools
import math

import jax
import jax.numpy as jnp
from jax import lax
from jax.experimental import pallas as pl
from jax.experimental.pallas import tpu as pltpu
from jax.sharding import PartitionSpec as P

QH = 64
KVH = 8
HD = 128
EPS = 1e-06
NEG = -1e30
MESH = pl.DeviceIdType.MESH
BLK = 128
ROWS = 8
SIDE = 4
PART = 4096
OWN = 1024
HEADS = 8
KT = 512
EARLY = (1,)
SCALE = 1.0 / math.sqrt(HD)
LOG2E = math.log2(math.e)
bf16 = jnp.bfloat16
f32 = jnp.float32


def dot_nt(a, b):
    return lax.dot_general(a, b, (((1,), (1,)), ((), ())), preferred_element_type=f32)


def dot_nn(a, b):
    return lax.dot_general(a, b, (((1,), (0,)), ((), ())), preferred_element_type=f32)


def fold(x, op):
    rows, cols = x.shape
    return op(x.reshape(rows // 8, 8, cols), axis=0)


def in_pairs(step, count):
    def pair(n, carry):
        step(2 * n, 2)
        return carry

    def single(n, carry):
        step(count - 1, 1)
        return carry

    def quad(n, carry):
        step(0, 4)
        return carry

    lax.fori_loop(0, count // 4, quad, 0)
    lax.fori_loop(0, count % 4 // 2, pair, 0)
    lax.fori_loop(0, count % 2, single, 0)


def kernel(
    q, k, v, do, seg, qg, kg,
    o, dq, dk, dv, qgp, kgp,
    qs, ds_, kv, kn, vn, kt_, vt_, os_, dqs, es, ms, firsts, dka, dva, sb, rb, fb, qn, ot, dqt, gacc, gb,
    s_in, r_in, s_kv, r_kv, s_ag, r_ag, s_out, r_out, s_rs, r_rs, s_f, r_f, s_g, r_g,
):
    seq = lax.axis_index("seq")
    dp = lax.axis_index("dp")
    x, y = seq // SIDE, seq % SIDE
    mine = (x, y)

    def own(p):
        return lax.select(p == 0, x, y)

    def remote(src, dst, ss, rs, dev):
        return pltpu.make_async_remote_copy(
            src_ref=src, dst_ref=dst, send_sem=ss, recv_sem=rs, device_id=dev, device_id_type=MESH
        )

    def cols(start, width):
        return pl.ds(pl.multiple_of(start, min(width, KT)), width)

    def dev_of(p, j):
        return (dp, j * SIDE + y) if p == 0 else (dp, x * SIDE + j)

    barrier = pltpu.get_barrier_semaphore()
    for p in (0, 1):
        for d in (1, 2, 3):
            pl.semaphore_signal(
                barrier, inc=1, device_id=dev_of(p, (mine[p] + d) % SIDE), device_id_type=MESH
            )
    for d in range(1, ROWS):
        pl.semaphore_signal(
            barrier, inc=1, device_id=((dp + d) % ROWS, seq), device_id_type=MESH
        )

    for p in (0, 1):
        me = mine[p]
        for i, src in enumerate((k, v)):
            pltpu.make_async_copy(
                src.at[:, cols(p * 512 + me * HD, HD)], kv.at[p, i, x, y], r_kv.at[p, i, me]
            ).start()
    pl.semaphore_wait(barrier, 6 + ROWS - 1)

    kv_sends = []
    for i, src in enumerate((k, v)):
        for d in (1, 3, 2):
            for p in (0, 1):
                me = mine[p]
                j = (me + d) % SIDE
                c = remote(
                    src.at[:, cols(p * 512 + j * HD, HD)], kv.at[p, i, x, y],
                    s_kv.at[p, i, d], r_kv.at[p, i, me], dev_of(p, j),
                )
                c.start()
                kv_sends.append(c)

    for p in (0, 1):
        me = mine[p]
        for i, src in enumerate((q, do)):
            dst = (qs, ds_)[i]
            pltpu.make_async_copy(
                src.at[:, cols(p * PART + me * OWN, OWN)], dst.at[p, me], r_in.at[i, p, me]
            ).start()

    ag_sends = []
    for i in (0, 1):
        for p in (0, 1):
            other = mine[1 - p]
            for j in range(SIDE):
                blk = kv.at[p, i, j, y] if p == 0 else kv.at[p, i, x, j]
                pltpu.make_async_copy(blk, blk, r_kv.at[p, i, j]).wait()
            held = kv.at[0, i, :, y] if p == 0 else kv.at[1, i, x]
            for d in (1, 3, 2):
                c = remote(
                    held, held, s_ag.at[p, i, d], r_ag.at[p, i, other],
                    dev_of(1 - p, (other + d) % SIDE),
                )
                c.start()
                ag_sends.append(c)

    in_sends = []

    def send_in(d):
        for p in (0, 1):
            me = mine[p]
            j = (me + d) % SIDE
            for i, src in enumerate((q, do)):
                dst = (qs, ds_)[i]
                c = remote(
                    src.at[:, cols(p * PART + j * OWN, OWN)], dst.at[p, me],
                    s_in.at[i, p, d], r_in.at[i, p, me], dev_of(p, j),
                )
                c.start()
                in_sends.append(c)

    for d in EARLY:
        send_in(d)

    ids = seg[dp]
    first = jnp.zeros((16, BLK), jnp.int32)
    for value in range(7):
        hits = jnp.where(ids == value, 1, 0)
        count = jnp.sum(jnp.sum(hits, axis=1, keepdims=True), axis=0, keepdims=True)
        first = first + jnp.where(ids > value, count, 0)
    seg_first = first

    dka[...] = jnp.zeros_like(dka)
    dva[...] = jnp.zeros_like(dva)
    gacc[...] = jnp.zeros_like(gacc)
    for i in range(16):
        firsts[i] = seg_first[i : i + 1, :]

    def prep(p, i, place):
        def block(n, carry):
            xb, yb = (n, place) if p == 0 else (place, n)
            rows = cols((xb * SIDE + yb) * BLK, BLK)
            if i == 0:
                raw = kv[p, 0, xb, yb].astype(f32)
                inv = lax.rsqrt(jnp.mean(raw * raw, axis=-1, keepdims=True) + EPS)
                normed = (raw * inv * kg[...]).astype(bf16)
                kn[p, rows, :] = normed
                kt_[p, :, rows] = normed.astype(f32).T.astype(bf16)
            else:
                val = kv[p, 1, xb, yb]
                vn[p, rows, :] = val
                vt_[p, :, rows] = val.astype(f32).T.astype(bf16)
            return carry

        lax.fori_loop(0, SIDE, block, 0)

    def gathered(i):
        for p in (0, 1):
            prep(p, i, mine[1 - p])
        for d in (1, 3, 2):
            for p in (0, 1):
                j = (mine[1 - p] + d) % SIDE
                blk = kv.at[0, i, :, j] if p == 0 else kv.at[1, i, j]
                pltpu.make_async_copy(blk, blk, r_ag.at[p, i, j]).wait()
                prep(p, i, j)

    gathered(0)
    for d in (1, 3, 2):
        if d not in EARLY:
            send_in(d)

    def share(p, i):
        acc = (dka, dva)[i]

        def pack(b, carry):
            sb[p, i, b // SIDE, b % SIDE] = acc[p, cols(b * BLK, BLK), :].astype(bf16)
            return carry

        lax.fori_loop(0, SIDE * SIDE, pack, 0)
        other = mine[1 - p]
        for d in (1, 3, 2):
            j = (other + d) % SIDE
            src = sb.at[0, i, :, j] if p == 0 else sb.at[1, i, j]
            remote(
                src, rb.at[p, other, i], s_rs.at[p, i, d], r_rs.at[p, i, other], dev_of(1 - p, j)
            ).start()

    last_of = (6, 7)

    def unit(u, carry):
        p = u % 2
        step = u // 2
        d = lax.select(step == 2, 3, lax.select(step == 3, 2, step))
        me = own(p)
        j = (me + d) % SIDE
        b = lax.select(p == 0, j * SIDE + y, x * SIDE + j)
        n_tiles = b // (KT // BLK) + 1
        for i, dst in enumerate((qs, ds_)):
            blk = dst.at[p, j]
            pltpu.make_async_copy(blk, blk, r_in.at[i, p, j]).wait()

        for h in range(HEADS):
            raw = qs[p, j, :, h * HD : (h + 1) * HD].astype(f32)
            inv = lax.rsqrt(jnp.mean(raw * raw, axis=-1, keepdims=True) + EPS)
            qn[0, h * BLK : (h + 1) * BLK, :] = (raw * inv * qg[...]).astype(bf16)
            qn[1, h * BLK : (h + 1) * BLK, :] = ds_[p, j, :, h * HD : (h + 1) * HD]

        q_pos = b * BLK + lax.broadcasted_iota(jnp.int32, (1, BLK), 1)
        q_first = firsts[b]

        def scores(first, tiles, carry):
            top, total = carry
            found = []
            for n in range(tiles):
                t = first + n
                s = dot_nt(kn[p, cols(t * KT, KT), :], qn[0])
                k_pos = t * KT + lax.broadcasted_iota(jnp.int32, (KT, BLK), 0)
                allowed = (k_pos >= q_first) & (k_pos <= q_pos)
                found.append(
                    jnp.concatenate(
                        [
                            jnp.where(allowed, s[:, h * BLK : (h + 1) * BLK], NEG)
                            for h in range(HEADS)
                        ],
                        axis=1,
                    )
                )
            new = top
            for s in found:
                new = jnp.maximum(new, jnp.max(fold(s, jnp.max), axis=0, keepdims=True))
            total = total * jnp.exp2((top - new) * (SCALE * LOG2E))
            for n in range(tiles):
                t, s = first + n, found[n]
                e = jnp.exp2((s - new) * (SCALE * LOG2E))
                es[cols(t * KT, KT), :] = e
                ms[t] = new
                total = total + fold(e, jnp.sum)
            return new, total

        carry_ = (jnp.full((1, OWN), NEG, f32), jnp.zeros((8, OWN), f32))
        carry_ = lax.fori_loop(0, n_tiles // 2, lambda n, c: scores(2 * n, 2, c), carry_)
        top, total = lax.fori_loop(
            0, n_tiles % 2, lambda n, c: scores(n_tiles - 1, 1, c), carry_
        )
        recip = 1.0 / jnp.sum(total, axis=0, keepdims=True)
        pl.when(u == 0)(functools.partial(gathered, 1))

        ot[...] = jnp.zeros_like(ot)

        def outs(first, tiles):
            rows = cols(first * KT, tiles * KT)
            parts = []
            for n in range(tiles):
                t = first + n
                factor = jnp.exp2((ms[t] - top) * (SCALE * LOG2E)) * recip
                parts.append((es[cols(t * KT, KT), :] * factor).astype(bf16))
            pr = jnp.concatenate(parts, axis=0)
            ot[...] += dot_nn(vt_[p, :, rows], pr)
            dva[p, rows, :] += dot_nn(pr, qn[1])

        in_pairs(outs, n_tiles)
        for part in (0, 1):
            pl.when(u == last_of[part])(functools.partial(share, part, 1))

        def send_out(i, src, dst):
            place = dst.at[:, cols(p * PART + me * OWN, OWN)]

            @pl.when(d == 0)
            def _():
                pltpu.make_async_copy(src.at[p, j], place, r_out.at[i, p, j]).start()

            @pl.when(d != 0)
            def _():
                remote(
                    src.at[p, j], place, s_out.at[i, p, d], r_out.at[i, p, me], (dp, b)
                ).start()

        ones = jnp.ones((8, HD), bf16)
        deltas = []
        for h in range(HEADS):
            out = ot[:, h * BLK : (h + 1) * BLK].T.astype(bf16)
            os_[p, j, :, h * HD : (h + 1) * HD] = out
            up = qn[1, h * BLK : (h + 1) * BLK, :].astype(f32)
            deltas.append(jnp.sum((up * out.astype(f32)).T, axis=0, keepdims=True))
        delta = jnp.concatenate(deltas, axis=1)
        send_out(0, os_, o)

        dqt[...] = jnp.zeros_like(dqt)

        def grads(first, tiles):
            rows = cols(first * KT, tiles * KT)
            parts = []
            for n in range(tiles):
                t = first + n
                own_rows = cols(t * KT, KT)
                dprob = dot_nt(vn[p, own_rows, :], qn[1])
                factor = jnp.exp2((ms[t] - top) * (SCALE * LOG2E)) * (recip * SCALE)
                parts.append(((es[own_rows, :] * factor) * (dprob - delta)).astype(bf16))
            g = jnp.concatenate(parts, axis=0)
            dqt[...] += dot_nn(kt_[p, :, rows], g)
            dka[p, rows, :] += dot_nn(g, qn[0])

        in_pairs(grads, n_tiles)
        for part in (0, 1):
            pl.when(u == last_of[part])(functools.partial(share, part, 0))

        for h in range(HEADS):
            raw = qs[p, j, :, h * HD : (h + 1) * HD].astype(f32)
            inv = lax.rsqrt(jnp.mean(raw * raw, axis=-1, keepdims=True) + EPS)
            hat = raw * inv
            grad = dqt[:, h * BLK : (h + 1) * BLK].T
            gacc[0] += fold(grad * hat, jnp.sum)
            g = grad * qg[...]
            dqs[p, j, :, h * HD : (h + 1) * HD] = (
                inv * (g - hat * jnp.mean(g * hat, axis=-1, keepdims=True))
            ).astype(bf16)

        send_out(1, dqs, dq)

        return carry

    lax.fori_loop(0, 8, unit, 0)

    def key_gain(t, carry):
        p, b = t // 16, t % 16
        raw = kv[p, 0, b // SIDE, b % SIDE].astype(f32)
        inv = lax.rsqrt(jnp.mean(raw * raw, axis=-1, keepdims=True) + EPS)
        gacc[1] += fold(dka[p, cols(b * BLK, BLK), :] * (raw * inv), jnp.sum)
        return carry

    lax.fori_loop(0, 32, key_gain, 0)

    g_sends = []
    stages = ((dp, ROWS), (x, SIDE), (y, SIDE))

    def gain_send(n, held):
        place, count = stages[n]
        gb[n, place] = held
        for d in range(1, count):
            j = (place + d) % count
            dev = (j, seq) if n == 0 else dev_of(n - 1, j)
            c = remote(gb.at[n, place], gb.at[n, place], s_g.at[n, d], r_g.at[n, place], dev)
            c.start()
            g_sends.append(c)

    def gain_sum(n):
        place, count = stages[n]
        for d in range(1, count):
            blk = gb.at[n, (place + d) % count]
            pltpu.make_async_copy(blk, blk, r_g.at[n, (place + d) % count]).wait()
        held = gb[n, 0]
        for j in range(1, count):
            held = held + gb[n, j]
        return held

    gain_send(
        0,
        jnp.concatenate(
            [jnp.sum(gacc[i], axis=0, keepdims=True) for i in (0, 1)]
            + [jnp.zeros((6, HD), f32)],
            axis=0,
        ),
    )
    gain_send(1, gain_sum(0))

    f_sends = []
    for p in (0, 1):
        other = mine[1 - p]
        me = mine[p]
        for d in (1, 3, 2):
            slot = (other + d) % SIDE
            for i in (0, 1):
                blk = rb.at[p, slot, i]
                pltpu.make_async_copy(blk, blk, r_rs.at[p, i, slot]).wait()
        for dd in (1, 3, 2, 0):
            j = (me + dd) % SIDE
            b = j * SIDE + y if p == 0 else x * SIDE + j
            rows = cols(b * BLK, BLK)
            kgrad = dka[p, rows, :]
            vgrad = dva[p, rows, :]
            for d in (1, 2, 3):
                slot = (other + d) % SIDE
                kgrad = kgrad + rb[p, slot, 0, j].astype(f32)
                vgrad = vgrad + rb[p, slot, 1, j].astype(f32)
            raw = (kv[0, 0, j, y] if p == 0 else kv[1, 0, x, j]).astype(f32)
            inv = lax.rsqrt(jnp.mean(raw * raw, axis=-1, keepdims=True) + EPS)
            hat = raw * inv
            g = kgrad * kg[...]
            fb[p, 0, j] = (inv * (g - hat * jnp.mean(g * hat, axis=-1, keepdims=True))).astype(
                bf16
            )
            fb[p, 1, j] = vgrad.astype(bf16)
            for i, dst in enumerate((dk, dv)):
                place = dst.at[:, cols(p * 512 + me * HD, HD)]
                if dd == 0:
                    pltpu.make_async_copy(fb.at[p, i, j], place, r_f.at[p, i, me]).start()
                else:
                    c = remote(
                        fb.at[p, i, j], place, s_f.at[p, i, dd], r_f.at[p, i, me], dev_of(p, j)
                    )
                    c.start()
                    f_sends.append(c)

    gain_send(2, gain_sum(1))
    held = gain_sum(2)
    tokens = ROWS * SIDE * SIDE * BLK
    qgp[...] = held[0:1] / math.sqrt(tokens * QH)
    kgp[...] = held[1:2] / math.sqrt(tokens * KVH)

    for c in kv_sends + ag_sends + in_sends + f_sends + g_sends:
        c.wait_send()

    def drain(t, carry):
        i, p, d = t // 6, (t // 3) % 2, t % 3 + 1
        src = os_.at[0, 0]
        pltpu.make_async_copy(src, src, s_out.at[i, p, d]).wait()
        return carry

    lax.fori_loop(0, 12, drain, 0)

    for p in (0, 1):
        for i in (0, 1):
            for d in (1, 2, 3):
                blk = rb.at[0, 0, 0]
                pltpu.make_async_copy(blk, blk, s_rs.at[p, i, d]).wait()

    def arrive(t, carry):
        i, p, j = t // 8, (t // 4) % 2, t % 4
        place = o.at[:, cols(p * PART + j * OWN, OWN)]
        pltpu.make_async_copy(place, place, r_out.at[i, p, j]).wait()
        return carry

    lax.fori_loop(0, 16, arrive, 0)
    for p in (0, 1):
        for i, dst in enumerate((dk, dv)):
            for j in range(SIDE):
                place = dst.at[:, cols(p * 512 + j * HD, HD)]
                pltpu.make_async_copy(place, place, r_f.at[p, i, j]).wait()


def on_device(q_proj, k_proj, v_proj, q_gain, k_gain, dout, segments):
    rows = q_proj.shape[0]
    ids = segments.reshape(ROWS, SIDE * SIDE, BLK)
    any_ = pl.BlockSpec(memory_space=pl.ANY)
    vmem = pl.BlockSpec(memory_space=pltpu.VMEM)
    dma = pltpu.SemaphoreType.DMA
    length = SIDE * SIDE * BLK
    o, dq, dk, dv, qgp, kgp = pl.pallas_call(
        kernel,
        out_shape=(
            jax.ShapeDtypeStruct((rows, QH * HD), bf16),
            jax.ShapeDtypeStruct((rows, QH * HD), bf16),
            jax.ShapeDtypeStruct((rows, KVH * HD), bf16),
            jax.ShapeDtypeStruct((rows, KVH * HD), bf16),
            jax.ShapeDtypeStruct((1, HD), f32),
            jax.ShapeDtypeStruct((1, HD), f32),
        ),
        in_specs=[any_, any_, any_, any_, vmem, vmem, vmem],
        out_specs=(any_, any_, any_, any_, vmem, vmem),
        scratch_shapes=[
            pltpu.VMEM((2, SIDE, BLK, OWN), bf16),
            pltpu.VMEM((2, SIDE, BLK, OWN), bf16),
            pltpu.VMEM((2, 2, SIDE, SIDE, BLK, HD), bf16),
            pltpu.VMEM((2, length, HD), bf16),
            pltpu.VMEM((2, length, HD), bf16),
            pltpu.VMEM((2, HD, length), bf16),
            pltpu.VMEM((2, HD, length), bf16),
            pltpu.VMEM((2, SIDE, BLK, OWN), bf16),
            pltpu.VMEM((2, SIDE, BLK, OWN), bf16),
            pltpu.VMEM((length, OWN), f32),
            pltpu.VMEM((SIDE, 1, OWN), f32),
            pltpu.VMEM((16, 1, BLK), jnp.int32),
            pltpu.VMEM((2, length, HD), f32),
            pltpu.VMEM((2, length, HD), f32),
            pltpu.VMEM((2, 2, SIDE, SIDE, BLK, HD), bf16),
            pltpu.VMEM((2, SIDE, 2, SIDE, BLK, HD), bf16),
            pltpu.VMEM((2, 2, SIDE, BLK, HD), bf16),
            pltpu.VMEM((2, OWN, HD), bf16),
            pltpu.VMEM((HD, OWN), f32),
            pltpu.VMEM((HD, OWN), f32),
            pltpu.VMEM((2, 8, HD), f32),
            pltpu.VMEM((3, ROWS, 8, HD), f32),
            dma((2, 2, SIDE)), dma((2, 2, SIDE)),
            dma((2, 2, SIDE)), dma((2, 2, SIDE)),
            dma((2, 2, SIDE)), dma((2, 2, SIDE)),
            dma((2, 2, SIDE)), dma((2, 2, SIDE)),
            dma((2, 2, SIDE)), dma((2, 2, SIDE)),
            dma((2, 2, SIDE)), dma((2, 2, SIDE)),
            dma((3, ROWS)), dma((3, ROWS)),
        ],
        name="exchange_attend",
        cost_estimate=pl.CostEstimate(
            flops=20_000_000_000, bytes_accessed=20_000_000, transcendentals=10_000_000
        ),
        compiler_params=pltpu.CompilerParams(
            collective_id=0, has_side_effects=True, vmem_limit_bytes=58 << 20
        ),
    )(q_proj, k_proj, v_proj, dout, ids, q_gain.reshape(1, HD), k_gain.reshape(1, HD))
    return o, dq, dk, dv, qgp.reshape(HD), kgp.reshape(HD)


def solution(mesh):
    split = P(("dp", "seq"), None)
    return jax.shard_map(
        on_device,
        mesh=mesh,
        in_specs=(split, split, split, P(), P(), split, P()),
        out_specs=(split, split, split, split, P(), P()),
        check_vma=False,
    )
```

```python
import functools
import math

import jax
import jax.numpy as jnp
from jax import lax
from jax.experimental import pallas as pl
from jax.experimental.pallas import tpu as pltpu
from jax.sharding import PartitionSpec as P

QH = 64
KVH = 8
HD = 128
EPS = 1e-06
NEG = -1e30
MESH = pl.DeviceIdType.MESH
BLK = 128
ROWS = 8
SIDE = 4
PART = 4096
OWN = 1024
HEADS = 8
KT = 512
EARLY = (1,)
SCALE = 1.0 / math.sqrt(HD)
LOG2E = math.log2(math.e)
bf16 = jnp.bfloat16
f32 = jnp.float32


def dot_nt(a, b):
    return lax.dot_general(a, b, (((1,), (1,)), ((), ())), preferred_element_type=f32)


def dot_nn(a, b):
    return lax.dot_general(a, b, (((1,), (0,)), ((), ())), preferred_element_type=f32)


def fold(x, op):
    rows, cols = x.shape
    return op(x.reshape(rows // 8, 8, cols), axis=0)


def in_pairs(step, count):
    def pair(n, carry):
        step(2 * n, 2)
        return carry

    def single(n, carry):
        step(count - 1, 1)
        return carry

    def quad(n, carry):
        step(0, 4)
        return carry

    lax.fori_loop(0, count // 4, quad, 0)
    lax.fori_loop(0, count % 4 // 2, pair, 0)
    lax.fori_loop(0, count % 2, single, 0)


def kernel(
    q, k, v, do, seg, qg, kg,
    o, dq, dk, dv, qgp, kgp,
    qs, ds_, kv, kn, vn, kt_, vt_, os_, dqs, es, ms, firsts, dka, dva, sb, rb, fb, qn, ot, dqt, gacc, gb,
    s_in, r_in, s_kv, r_kv, s_ag, r_ag, s_out, r_out, s_rs, r_rs, s_f, r_f, s_g, r_g,
):
    seq = lax.axis_index("seq")
    dp = lax.axis_index("dp")
    x, y = seq // SIDE, seq % SIDE
    mine = (x, y)

    def own(p):
        return lax.select(p == 0, x, y)

    def remote(src, dst, ss, rs, dev):
        return pltpu.make_async_remote_copy(
            src_ref=src, dst_ref=dst, send_sem=ss, recv_sem=rs, device_id=dev, device_id_type=MESH
        )

    def cols(start, width):
        return pl.ds(pl.multiple_of(start, min(width, KT)), width)

    def dev_of(p, j):
        return (dp, j * SIDE + y) if p == 0 else (dp, x * SIDE + j)

    barrier = pltpu.get_barrier_semaphore()
    for p in (0, 1):
        for d in (1, 2, 3):
            pl.semaphore_signal(
                barrier, inc=1, device_id=dev_of(p, (mine[p] + d) % SIDE), device_id_type=MESH
            )
    for d in range(1, ROWS):
        pl.semaphore_signal(
            barrier, inc=1, device_id=((dp + d) % ROWS, seq), device_id_type=MESH
        )

    for p in (0, 1):
        me = mine[p]
        for i, src in enumerate((k, v)):
            pltpu.make_async_copy(
                src.at[:, cols(p * 512 + me * HD, HD)], kv.at[p, i, x, y], r_kv.at[p, i, me]
            ).start()
    pl.semaphore_wait(barrier, 6 + ROWS - 1)

    kv_sends = []
    for i, src in enumerate((k, v)):
        for d in (1, 3, 2):
            for p in (0, 1):
                me = mine[p]
                j = (me + d) % SIDE
                c = remote(
                    src.at[:, cols(p * 512 + j * HD, HD)], kv.at[p, i, x, y],
                    s_kv.at[p, i, d], r_kv.at[p, i, me], dev_of(p, j),
                )
                c.start()
                kv_sends.append(c)

    for p in (0, 1):
        me = mine[p]
        for i, src in enumerate((q, do)):
            dst = (qs, ds_)[i]
            pltpu.make_async_copy(
                src.at[:, cols(p * PART + me * OWN, OWN)], dst.at[p, me], r_in.at[i, p, me]
            ).start()

    ag_sends = []
    for i in (0, 1):
        for p in (0, 1):
            other = mine[1 - p]
            for j in range(SIDE):
                blk = kv.at[p, i, j, y] if p == 0 else kv.at[p, i, x, j]
                pltpu.make_async_copy(blk, blk, r_kv.at[p, i, j]).wait()
            held = kv.at[0, i, :, y] if p == 0 else kv.at[1, i, x]
            for d in (1, 3, 2):
                c = remote(
                    held, held, s_ag.at[p, i, d], r_ag.at[p, i, other],
                    dev_of(1 - p, (other + d) % SIDE),
                )
                c.start()
                ag_sends.append(c)

    in_sends = []

    def send_in(d):
        for p in (0, 1):
            me = mine[p]
            j = (me + d) % SIDE
            for i, src in enumerate((q, do)):
                dst = (qs, ds_)[i]
                c = remote(
                    src.at[:, cols(p * PART + j * OWN, OWN)], dst.at[p, me],
                    s_in.at[i, p, d], r_in.at[i, p, me], dev_of(p, j),
                )
                c.start()
                in_sends.append(c)

    for d in EARLY:
        send_in(d)

    ids = seg[dp]
    first = jnp.zeros((16, BLK), jnp.int32)
    for value in range(7):
        hits = jnp.where(ids == value, 1, 0)
        count = jnp.sum(jnp.sum(hits, axis=1, keepdims=True), axis=0, keepdims=True)
        first = first + jnp.where(ids > value, count, 0)
    seg_first = first

    dka[...] = jnp.zeros_like(dka)
    dva[...] = jnp.zeros_like(dva)
    gacc[...] = jnp.zeros_like(gacc)
    for i in range(16):
        firsts[i] = seg_first[i : i + 1, :]

    def prep(p, i, place):
        def block(n, carry):
            xb, yb = (n, place) if p == 0 else (place, n)
            rows = cols((xb * SIDE + yb) * BLK, BLK)
            if i == 0:
                raw = kv[p, 0, xb, yb].astype(f32)
                inv = lax.rsqrt(jnp.mean(raw * raw, axis=-1, keepdims=True) + EPS)
                normed = (raw * inv * kg[...]).astype(bf16)
                kn[p, rows, :] = normed
                kt_[p, :, rows] = normed.astype(f32).T.astype(bf16)
            else:
                val = kv[p, 1, xb, yb]
                vn[p, rows, :] = val
                vt_[p, :, rows] = val.astype(f32).T.astype(bf16)
            return carry

        lax.fori_loop(0, SIDE, block, 0)

    def gathered(i):
        for p in (0, 1):
            prep(p, i, mine[1 - p])
        for d in (1, 3, 2):
            for p in (0, 1):
                j = (mine[1 - p] + d) % SIDE
                blk = kv.at[0, i, :, j] if p == 0 else kv.at[1, i, j]
                pltpu.make_async_copy(blk, blk, r_ag.at[p, i, j]).wait()
                prep(p, i, j)

    gathered(0)
    for d in (1, 3, 2):
        if d not in EARLY:
            send_in(d)

    def share(p, i):
        acc = (dka, dva)[i]

        def pack(b, carry):
            sb[p, i, b // SIDE, b % SIDE] = acc[p, cols(b * BLK, BLK), :].astype(bf16)
            return carry

        lax.fori_loop(0, SIDE * SIDE, pack, 0)
        other = mine[1 - p]
        for d in (1, 3, 2):
            j = (other + d) % SIDE
            src = sb.at[0, i, :, j] if p == 0 else sb.at[1, i, j]
            remote(
                src, rb.at[p, other, i], s_rs.at[p, i, d], r_rs.at[p, i, other], dev_of(1 - p, j)
            ).start()

    last_of = (6, 7)

    def unit(u, carry):
        p = u % 2
        step = u // 2
        d = lax.select(step == 2, 3, lax.select(step == 3, 2, step))
        me = own(p)
        j = (me + d) % SIDE
        b = lax.select(p == 0, j * SIDE + y, x * SIDE + j)
        n_tiles = b // (KT // BLK) + 1
        for i, dst in enumerate((qs, ds_)):
            blk = dst.at[p, j]
            pltpu.make_async_copy(blk, blk, r_in.at[i, p, j]).wait()

        for h in range(HEADS):
            raw = qs[p, j, :, h * HD : (h + 1) * HD].astype(f32)
            inv = lax.rsqrt(jnp.mean(raw * raw, axis=-1, keepdims=True) + EPS)
            qn[0, h * BLK : (h + 1) * BLK, :] = (raw * inv * qg[...]).astype(bf16)
            qn[1, h * BLK : (h + 1) * BLK, :] = ds_[p, j, :, h * HD : (h + 1) * HD]

        q_pos = b * BLK + lax.broadcasted_iota(jnp.int32, (1, BLK), 1)
        q_first = firsts[b]

        def scores(first, tiles, carry):
            top, total = carry
            found = []
            for n in range(tiles):
                t = first + n
                s = dot_nt(kn[p, cols(t * KT, KT), :], qn[0])
                k_pos = t * KT + lax.broadcasted_iota(jnp.int32, (KT, BLK), 0)
                allowed = (k_pos >= q_first) & (k_pos <= q_pos)
                found.append(
                    jnp.concatenate(
                        [
                            jnp.where(allowed, s[:, h * BLK : (h + 1) * BLK], NEG)
                            for h in range(HEADS)
                        ],
                        axis=1,
                    )
                )
            new = top
            for s in found:
                new = jnp.maximum(new, jnp.max(fold(s, jnp.max), axis=0, keepdims=True))
            total = total * jnp.exp2((top - new) * (SCALE * LOG2E))
            for n in range(tiles):
                t, s = first + n, found[n]
                e = jnp.exp2((s - new) * (SCALE * LOG2E))
                es[cols(t * KT, KT), :] = e
                ms[t] = new
                total = total + fold(e, jnp.sum)
            return new, total

        carry_ = (jnp.full((1, OWN), NEG, f32), jnp.zeros((8, OWN), f32))
        carry_ = lax.fori_loop(0, n_tiles // 4, lambda n, c: scores(0, 4, c), carry_)
        carry_ = lax.fori_loop(0, n_tiles % 4 // 2, lambda n, c: scores(0, 2, c), carry_)
        top, total = lax.fori_loop(
            0, n_tiles % 2, lambda n, c: scores(n_tiles - 1, 1, c), carry_
        )
        recip = 1.0 / jnp.sum(total, axis=0, keepdims=True)
        pl.when(u == 0)(functools.partial(gathered, 1))

        ot[...] = jnp.zeros_like(ot)

        def outs(first, tiles):
            rows = cols(first * KT, tiles * KT)
            parts = []
            for n in range(tiles):
                t = first + n
                factor = jnp.exp2((ms[t] - top) * (SCALE * LOG2E)) * recip
                parts.append((es[cols(t * KT, KT), :] * factor).astype(bf16))
            pr = jnp.concatenate(parts, axis=0)
            ot[...] += dot_nn(vt_[p, :, rows], pr)
            dva[p, rows, :] += dot_nn(pr, qn[1])

        in_pairs(outs, n_tiles)
        for part in (0, 1):
            pl.when(u == last_of[part])(functools.partial(share, part, 1))

        def send_out(i, src, dst):
            place = dst.at[:, cols(p * PART + me * OWN, OWN)]

            @pl.when(d == 0)
            def _():
                pltpu.make_async_copy(src.at[p, j], place, r_out.at[i, p, j]).start()

            @pl.when(d != 0)
            def _():
                remote(
                    src.at[p, j], place, s_out.at[i, p, d], r_out.at[i, p, me], (dp, b)
                ).start()

        ones = jnp.ones((8, HD), bf16)
        deltas = []
        for h in range(HEADS):
            out = ot[:, h * BLK : (h + 1) * BLK].T.astype(bf16)
            os_[p, j, :, h * HD : (h + 1) * HD] = out
            up = qn[1, h * BLK : (h + 1) * BLK, :].astype(f32)
            deltas.append(jnp.sum((up * out.astype(f32)).T, axis=0, keepdims=True))
        delta = jnp.concatenate(deltas, axis=1)
        send_out(0, os_, o)

        dqt[...] = jnp.zeros_like(dqt)

        def grads(first, tiles):
            rows = cols(first * KT, tiles * KT)
            parts = []
            for n in range(tiles):
                t = first + n
                own_rows = cols(t * KT, KT)
                dprob = dot_nt(vn[p, own_rows, :], qn[1])
                factor = jnp.exp2((ms[t] - top) * (SCALE * LOG2E)) * (recip * SCALE)
                parts.append(((es[own_rows, :] * factor) * (dprob - delta)).astype(bf16))
            g = jnp.concatenate(parts, axis=0)
            dqt[...] += dot_nn(kt_[p, :, rows], g)
            dka[p, rows, :] += dot_nn(g, qn[0])

        in_pairs(grads, n_tiles)
        for part in (0, 1):
            pl.when(u == last_of[part])(functools.partial(share, part, 0))

        for h in range(HEADS):
            raw = qs[p, j, :, h * HD : (h + 1) * HD].astype(f32)
            inv = lax.rsqrt(jnp.mean(raw * raw, axis=-1, keepdims=True) + EPS)
            hat = raw * inv
            grad = dqt[:, h * BLK : (h + 1) * BLK].T
            gacc[0] += fold(grad * hat, jnp.sum)
            g = grad * qg[...]
            dqs[p, j, :, h * HD : (h + 1) * HD] = (
                inv * (g - hat * jnp.mean(g * hat, axis=-1, keepdims=True))
            ).astype(bf16)

        send_out(1, dqs, dq)

        return carry

    lax.fori_loop(0, 8, unit, 0)

    def key_gain(t, carry):
        p, b = t // 16, t % 16
        raw = kv[p, 0, b // SIDE, b % SIDE].astype(f32)
        inv = lax.rsqrt(jnp.mean(raw * raw, axis=-1, keepdims=True) + EPS)
        gacc[1] += fold(dka[p, cols(b * BLK, BLK), :] * (raw * inv), jnp.sum)
        return carry

    lax.fori_loop(0, 32, key_gain, 0)

    g_sends = []
    stages = ((dp, ROWS), (x, SIDE), (y, SIDE))

    def gain_send(n, held):
        place, count = stages[n]
        gb[n, place] = held
        for d in range(1, count):
            j = (place + d) % count
            dev = (j, seq) if n == 0 else dev_of(n - 1, j)
            c = remote(gb.at[n, place], gb.at[n, place], s_g.at[n, d], r_g.at[n, place], dev)
            c.start()
            g_sends.append(c)

    def gain_sum(n):
        place, count = stages[n]
        for d in range(1, count):
            blk = gb.at[n, (place + d) % count]
            pltpu.make_async_copy(blk, blk, r_g.at[n, (place + d) % count]).wait()
        held = gb[n, 0]
        for j in range(1, count):
            held = held + gb[n, j]
        return held

    gain_send(
        0,
        jnp.concatenate(
            [jnp.sum(gacc[i], axis=0, keepdims=True) for i in (0, 1)]
            + [jnp.zeros((6, HD), f32)],
            axis=0,
        ),
    )
    gain_send(1, gain_sum(0))

    f_sends = []
    for p in (0, 1):
        other = mine[1 - p]
        me = mine[p]
        for d in (1, 3, 2):
            slot = (other + d) % SIDE
            for i in (0, 1):
                blk = rb.at[p, slot, i]
                pltpu.make_async_copy(blk, blk, r_rs.at[p, i, slot]).wait()
        for dd in (1, 3, 2, 0):
            j = (me + dd) % SIDE
            b = j * SIDE + y if p == 0 else x * SIDE + j
            rows = cols(b * BLK, BLK)
            kgrad = dka[p, rows, :]
            vgrad = dva[p, rows, :]
            for d in (1, 2, 3):
                slot = (other + d) % SIDE
                kgrad = kgrad + rb[p, slot, 0, j].astype(f32)
                vgrad = vgrad + rb[p, slot, 1, j].astype(f32)
            raw = (kv[0, 0, j, y] if p == 0 else kv[1, 0, x, j]).astype(f32)
            inv = lax.rsqrt(jnp.mean(raw * raw, axis=-1, keepdims=True) + EPS)
            hat = raw * inv
            g = kgrad * kg[...]
            fb[p, 0, j] = (inv * (g - hat * jnp.mean(g * hat, axis=-1, keepdims=True))).astype(
                bf16
            )
            fb[p, 1, j] = vgrad.astype(bf16)
            for i, dst in enumerate((dk, dv)):
                place = dst.at[:, cols(p * 512 + me * HD, HD)]
                if dd == 0:
                    pltpu.make_async_copy(fb.at[p, i, j], place, r_f.at[p, i, me]).start()
                else:
                    c = remote(
                        fb.at[p, i, j], place, s_f.at[p, i, dd], r_f.at[p, i, me], dev_of(p, j)
                    )
                    c.start()
                    f_sends.append(c)

    gain_send(2, gain_sum(1))
    held = gain_sum(2)
    tokens = ROWS * SIDE * SIDE * BLK
    qgp[...] = held[0:1] / math.sqrt(tokens * QH)
    kgp[...] = held[1:2] / math.sqrt(tokens * KVH)

    for c in kv_sends + ag_sends + in_sends + f_sends + g_sends:
        c.wait_send()

    def drain(t, carry):
        i, p, d = t // 6, (t // 3) % 2, t % 3 + 1
        src = os_.at[0, 0]
        pltpu.make_async_copy(src, src, s_out.at[i, p, d]).wait()
        return carry

    lax.fori_loop(0, 12, drain, 0)

    for p in (0, 1):
        for i in (0, 1):
            for d in (1, 2, 3):
                blk = rb.at[0, 0, 0]
                pltpu.make_async_copy(blk, blk, s_rs.at[p, i, d]).wait()

    def arrive(t, carry):
        i, p, j = t // 8, (t // 4) % 2, t % 4
        place = o.at[:, cols(p * PART + j * OWN, OWN)]
        pltpu.make_async_copy(place, place, r_out.at[i, p, j]).wait()
        return carry

    lax.fori_loop(0, 16, arrive, 0)
    for p in (0, 1):
        for i, dst in enumerate((dk, dv)):
            for j in range(SIDE):
                place = dst.at[:, cols(p * 512 + j * HD, HD)]
                pltpu.make_async_copy(place, place, r_f.at[p, i, j]).wait()


def on_device(q_proj, k_proj, v_proj, q_gain, k_gain, dout, segments):
    rows = q_proj.shape[0]
    ids = segments.reshape(ROWS, SIDE * SIDE, BLK)
    any_ = pl.BlockSpec(memory_space=pl.ANY)
    vmem = pl.BlockSpec(memory_space=pltpu.VMEM)
    dma = pltpu.SemaphoreType.DMA
    length = SIDE * SIDE * BLK
    o, dq, dk, dv, qgp, kgp = pl.pallas_call(
        kernel,
        out_shape=(
            jax.ShapeDtypeStruct((rows, QH * HD), bf16),
            jax.ShapeDtypeStruct((rows, QH * HD), bf16),
            jax.ShapeDtypeStruct((rows, KVH * HD), bf16),
            jax.ShapeDtypeStruct((rows, KVH * HD), bf16),
            jax.ShapeDtypeStruct((1, HD), f32),
            jax.ShapeDtypeStruct((1, HD), f32),
        ),
        in_specs=[any_, any_, any_, any_, vmem, vmem, vmem],
        out_specs=(any_, any_, any_, any_, vmem, vmem),
        scratch_shapes=[
            pltpu.VMEM((2, SIDE, BLK, OWN), bf16),
            pltpu.VMEM((2, SIDE, BLK, OWN), bf16),
            pltpu.VMEM((2, 2, SIDE, SIDE, BLK, HD), bf16),
            pltpu.VMEM((2, length, HD), bf16),
            pltpu.VMEM((2, length, HD), bf16),
            pltpu.VMEM((2, HD, length), bf16),
            pltpu.VMEM((2, HD, length), bf16),
            pltpu.VMEM((2, SIDE, BLK, OWN), bf16),
            pltpu.VMEM((2, SIDE, BLK, OWN), bf16),
            pltpu.VMEM((length, OWN), f32),
            pltpu.VMEM((SIDE, 1, OWN), f32),
            pltpu.VMEM((16, 1, BLK), jnp.int32),
            pltpu.VMEM((2, length, HD), f32),
            pltpu.VMEM((2, length, HD), f32),
            pltpu.VMEM((2, 2, SIDE, SIDE, BLK, HD), bf16),
            pltpu.VMEM((2, SIDE, 2, SIDE, BLK, HD), bf16),
            pltpu.VMEM((2, 2, SIDE, BLK, HD), bf16),
            pltpu.VMEM((2, OWN, HD), bf16),
            pltpu.VMEM((HD, OWN), f32),
            pltpu.VMEM((HD, OWN), f32),
            pltpu.VMEM((2, 8, HD), f32),
            pltpu.VMEM((3, ROWS, 8, HD), f32),
            dma((2, 2, SIDE)), dma((2, 2, SIDE)),
            dma((2, 2, SIDE)), dma((2, 2, SIDE)),
            dma((2, 2, SIDE)), dma((2, 2, SIDE)),
            dma((2, 2, SIDE)), dma((2, 2, SIDE)),
            dma((2, 2, SIDE)), dma((2, 2, SIDE)),
            dma((2, 2, SIDE)), dma((2, 2, SIDE)),
            dma((3, ROWS)), dma((3, ROWS)),
        ],
        name="exchange_attend",
        cost_estimate=pl.CostEstimate(
            flops=20_000_000_000, bytes_accessed=20_000_000, transcendentals=10_000_000
        ),
        compiler_params=pltpu.CompilerParams(
            collective_id=0, has_side_effects=True, vmem_limit_bytes=58 << 20
        ),
    )(q_proj, k_proj, v_proj, dout, ids, q_gain.reshape(1, HD), k_gain.reshape(1, HD))
    return o, dq, dk, dv, qgp.reshape(HD), kgp.reshape(HD)


def solution(mesh):
    split = P(("dp", "seq"), None)
    return jax.shard_map(
        on_device,
        mesh=mesh,
        in_specs=(split, split, split, P(), P(), split, P()),
        out_specs=(split, split, split, split, P(), P()),
        check_vma=False,
    )
```

```python
import functools
import math

import jax
import jax.numpy as jnp
from jax import lax
from jax.experimental import pallas as pl
from jax.experimental.pallas import tpu as pltpu
from jax.sharding import PartitionSpec as P

QH = 64
KVH = 8
HD = 128
EPS = 1e-06
NEG = -1e30
MESH = pl.DeviceIdType.MESH
BLK = 128
ROWS = 8
SIDE = 4
PART = 4096
OWN = 1024
HEADS = 8
KT = 512
EARLY = (1,)
SCALE = 1.0 / math.sqrt(HD)
LOG2E = math.log2(math.e)
bf16 = jnp.bfloat16
f32 = jnp.float32


def dot_nt(a, b):
    return lax.dot_general(a, b, (((1,), (1,)), ((), ())), preferred_element_type=f32)


def dot_nn(a, b):
    return lax.dot_general(a, b, (((1,), (0,)), ((), ())), preferred_element_type=f32)


def fold(x, op):
    rows, cols = x.shape
    return op(x.reshape(rows // 8, 8, cols), axis=0)


def in_pairs(step, count):
    def pair(n, carry):
        step(2 * n, 2)
        return carry

    def single(n, carry):
        step(count - 1, 1)
        return carry

    def quad(n, carry):
        step(0, 4)
        return carry

    lax.fori_loop(0, count // 4, quad, 0)
    lax.fori_loop(0, count % 4 // 2, pair, 0)
    lax.fori_loop(0, count % 2, single, 0)


def kernel(
    q, k, v, do, seg, qg, kg,
    o, dq, dk, dv, qgp, kgp,
    qs, ds_, kv, kn, vn, kt_, vt_, os_, dqs, es, ms, firsts, dka, dva, sb, rb, fb, qn, ot, dqt, gacc, gb,
    s_in, r_in, s_kv, r_kv, s_ag, r_ag, s_out, r_out, s_rs, r_rs, s_f, r_f, s_g, r_g,
):
    seq = lax.axis_index("seq")
    dp = lax.axis_index("dp")
    x, y = seq // SIDE, seq % SIDE
    mine = (x, y)

    def own(p):
        return lax.select(p == 0, x, y)

    def remote(src, dst, ss, rs, dev):
        return pltpu.make_async_remote_copy(
            src_ref=src, dst_ref=dst, send_sem=ss, recv_sem=rs, device_id=dev, device_id_type=MESH
        )

    def cols(start, width):
        return pl.ds(pl.multiple_of(start, min(width, KT)), width)

    def dev_of(p, j):
        return (dp, j * SIDE + y) if p == 0 else (dp, x * SIDE + j)

    barrier = pltpu.get_barrier_semaphore()
    for p in (0, 1):
        for d in (1, 2, 3):
            pl.semaphore_signal(
                barrier, inc=1, device_id=dev_of(p, (mine[p] + d) % SIDE), device_id_type=MESH
            )
    for d in range(1, ROWS):
        pl.semaphore_signal(
            barrier, inc=1, device_id=((dp + d) % ROWS, seq), device_id_type=MESH
        )

    for p in (0, 1):
        me = mine[p]
        for i, src in enumerate((k, v)):
            pltpu.make_async_copy(
                src.at[:, cols(p * 512 + me * HD, HD)], kv.at[p, i, x, y], r_kv.at[p, i, me]
            ).start()
    pl.semaphore_wait(barrier, 6 + ROWS - 1)

    kv_sends = []
    for i, src in enumerate((k, v)):
        for d in (1, 3, 2):
            for p in (0, 1):
                me = mine[p]
                j = (me + d) % SIDE
                c = remote(
                    src.at[:, cols(p * 512 + j * HD, HD)], kv.at[p, i, x, y],
                    s_kv.at[p, i, d], r_kv.at[p, i, me], dev_of(p, j),
                )
                c.start()
                kv_sends.append(c)

    for p in (0, 1):
        me = mine[p]
        for i, src in enumerate((q, do)):
            dst = (qs, ds_)[i]
            pltpu.make_async_copy(
                src.at[:, cols(p * PART + me * OWN, OWN)], dst.at[p, me], r_in.at[i, p, me]
            ).start()

    ag_sends = []
    for i in (0, 1):
        for p in (0, 1):
            other = mine[1 - p]
            for j in range(SIDE):
                blk = kv.at[p, i, j, y] if p == 0 else kv.at[p, i, x, j]
                pltpu.make_async_copy(blk, blk, r_kv.at[p, i, j]).wait()
            held = kv.at[0, i, :, y] if p == 0 else kv.at[1, i, x]
            for d in (1, 3, 2):
                c = remote(
                    held, held, s_ag.at[p, i, d], r_ag.at[p, i, other],
                    dev_of(1 - p, (other + d) % SIDE),
                )
                c.start()
                ag_sends.append(c)

    def send_in(d):
        for p in (0, 1):
            me = mine[p]
            j = (me + d) % SIDE
            for i, src in enumerate((q, do)):
                dst = (qs, ds_)[i]
                c = remote(
                    src.at[:, cols(p * PART + j * OWN, OWN)], dst.at[p, me],
                    s_in.at[i, p, d], r_in.at[i, p, me], dev_of(p, j),
                )
                c.start()

    for d in EARLY:
        send_in(d)

    ids = seg[dp]
    first = jnp.zeros((16, BLK), jnp.int32)
    for value in range(7):
        hits = jnp.where(ids == value, 1, 0)
        count = jnp.sum(jnp.sum(hits, axis=1, keepdims=True), axis=0, keepdims=True)
        first = first + jnp.where(ids > value, count, 0)
    seg_first = first

    dka[...] = jnp.zeros_like(dka)
    dva[...] = jnp.zeros_like(dva)
    gacc[...] = jnp.zeros_like(gacc)
    for i in range(16):
        firsts[i] = seg_first[i : i + 1, :]

    def prep(p, i, place):
        def block(n, carry):
            xb, yb = (n, place) if p == 0 else (place, n)
            rows = cols((xb * SIDE + yb) * BLK, BLK)
            if i == 0:
                raw = kv[p, 0, xb, yb].astype(f32)
                inv = lax.rsqrt(jnp.mean(raw * raw, axis=-1, keepdims=True) + EPS)
                normed = (raw * inv * kg[...]).astype(bf16)
                kn[p, rows, :] = normed
                kt_[p, :, rows] = normed.astype(f32).T.astype(bf16)
            else:
                val = kv[p, 1, xb, yb]
                vn[p, rows, :] = val
                vt_[p, :, rows] = val.astype(f32).T.astype(bf16)
            return carry

        lax.fori_loop(0, SIDE, block, 0)

    def gathered(i):
        for p in (0, 1):
            prep(p, i, mine[1 - p])
        for d in (1, 3, 2):
            for p in (0, 1):
                j = (mine[1 - p] + d) % SIDE
                blk = kv.at[0, i, :, j] if p == 0 else kv.at[1, i, j]
                pltpu.make_async_copy(blk, blk, r_ag.at[p, i, j]).wait()
                prep(p, i, j)

    gathered(0)

    def share(p, i):
        acc = (dka, dva)[i]

        def pack(b, carry):
            sb[p, i, b // SIDE, b % SIDE] = acc[p, cols(b * BLK, BLK), :].astype(bf16)
            return carry

        lax.fori_loop(0, SIDE * SIDE, pack, 0)
        other = mine[1 - p]
        for d in (1, 3, 2):
            j = (other + d) % SIDE
            src = sb.at[0, i, :, j] if p == 0 else sb.at[1, i, j]
            remote(
                src, rb.at[p, other, i], s_rs.at[p, i, d], r_rs.at[p, i, other], dev_of(1 - p, j)
            ).start()

    last_of = (6, 7)

    def unit(u, carry):
        p = u % 2
        step = u // 2
        d = lax.select(step == 2, 3, lax.select(step == 3, 2, step))
        me = own(p)
        j = (me + d) % SIDE
        b = lax.select(p == 0, j * SIDE + y, x * SIDE + j)
        n_tiles = b // (KT // BLK) + 1
        for i, dst in enumerate((qs, ds_)):
            blk = dst.at[p, j]
            pltpu.make_async_copy(blk, blk, r_in.at[i, p, j]).wait()

        for h in range(HEADS):
            raw = qs[p, j, :, h * HD : (h + 1) * HD].astype(f32)
            inv = lax.rsqrt(jnp.mean(raw * raw, axis=-1, keepdims=True) + EPS)
            qn[0, h * BLK : (h + 1) * BLK, :] = (raw * inv * qg[...]).astype(bf16)
            qn[1, h * BLK : (h + 1) * BLK, :] = ds_[p, j, :, h * HD : (h + 1) * HD]

        q_pos = b * BLK + lax.broadcasted_iota(jnp.int32, (1, BLK), 1)
        q_first = firsts[b]

        def scores(first, tiles, carry):
            top, total = carry
            found = []
            for n in range(tiles):
                t = first + n
                s = dot_nt(kn[p, cols(t * KT, KT), :], qn[0])
                k_pos = t * KT + lax.broadcasted_iota(jnp.int32, (KT, BLK), 0)
                allowed = (k_pos >= q_first) & (k_pos <= q_pos)
                found.append(
                    jnp.concatenate(
                        [
                            jnp.where(allowed, s[:, h * BLK : (h + 1) * BLK], NEG)
                            for h in range(HEADS)
                        ],
                        axis=1,
                    )
                )
            new = top
            for s in found:
                new = jnp.maximum(new, jnp.max(fold(s, jnp.max), axis=0, keepdims=True))
            total = total * jnp.exp2((top - new) * (SCALE * LOG2E))
            for n in range(tiles):
                t, s = first + n, found[n]
                e = jnp.exp2((s - new) * (SCALE * LOG2E))
                es[cols(t * KT, KT), :] = e
                ms[t] = new
                total = total + fold(e, jnp.sum)
            return new, total

        carry_ = (jnp.full((1, OWN), NEG, f32), jnp.zeros((8, OWN), f32))
        carry_ = lax.fori_loop(0, n_tiles // 4, lambda n, c: scores(0, 4, c), carry_)
        carry_ = lax.fori_loop(0, n_tiles % 4 // 2, lambda n, c: scores(0, 2, c), carry_)
        top, total = lax.fori_loop(
            0, n_tiles % 2, lambda n, c: scores(n_tiles - 1, 1, c), carry_
        )
        recip = 1.0 / jnp.sum(total, axis=0, keepdims=True)

        @pl.when(u == 0)
        def _():
            gathered(1)
            for d in (3, 2):
                send_in(d)


        ot[...] = jnp.zeros_like(ot)

        def outs(first, tiles):
            rows = cols(first * KT, tiles * KT)
            parts = []
            for n in range(tiles):
                t = first + n
                factor = jnp.exp2((ms[t] - top) * (SCALE * LOG2E)) * recip
                parts.append((es[cols(t * KT, KT), :] * factor).astype(bf16))
            pr = jnp.concatenate(parts, axis=0)
            ot[...] += dot_nn(vt_[p, :, rows], pr)
            dva[p, rows, :] += dot_nn(pr, qn[1])

        in_pairs(outs, n_tiles)
        for part in (0, 1):
            pl.when(u == last_of[part])(functools.partial(share, part, 1))

        def send_out(i, src, dst):
            place = dst.at[:, cols(p * PART + me * OWN, OWN)]

            @pl.when(d == 0)
            def _():
                pltpu.make_async_copy(src.at[p, j], place, r_out.at[i, p, j]).start()

            @pl.when(d != 0)
            def _():
                remote(
                    src.at[p, j], place, s_out.at[i, p, d], r_out.at[i, p, me], (dp, b)
                ).start()

        ones = jnp.ones((8, HD), bf16)
        deltas = []
        for h in range(HEADS):
            out = ot[:, h * BLK : (h + 1) * BLK].T.astype(bf16)
            os_[p, j, :, h * HD : (h + 1) * HD] = out
            up = qn[1, h * BLK : (h + 1) * BLK, :].astype(f32)
            deltas.append(jnp.sum((up * out.astype(f32)).T, axis=0, keepdims=True))
        delta = jnp.concatenate(deltas, axis=1)
        send_out(0, os_, o)

        dqt[...] = jnp.zeros_like(dqt)

        def grads(first, tiles):
            rows = cols(first * KT, tiles * KT)
            parts = []
            for n in range(tiles):
                t = first + n
                own_rows = cols(t * KT, KT)
                dprob = dot_nt(vn[p, own_rows, :], qn[1])
                factor = jnp.exp2((ms[t] - top) * (SCALE * LOG2E)) * (recip * SCALE)
                parts.append(((es[own_rows, :] * factor) * (dprob - delta)).astype(bf16))
            g = jnp.concatenate(parts, axis=0)
            dqt[...] += dot_nn(kt_[p, :, rows], g)
            dka[p, rows, :] += dot_nn(g, qn[0])

        in_pairs(grads, n_tiles)
        for part in (0, 1):
            pl.when(u == last_of[part])(functools.partial(share, part, 0))

        for h in range(HEADS):
            raw = qs[p, j, :, h * HD : (h + 1) * HD].astype(f32)
            inv = lax.rsqrt(jnp.mean(raw * raw, axis=-1, keepdims=True) + EPS)
            hat = raw * inv
            grad = dqt[:, h * BLK : (h + 1) * BLK].T
            gacc[0] += fold(grad * hat, jnp.sum)
            g = grad * qg[...]
            dqs[p, j, :, h * HD : (h + 1) * HD] = (
                inv * (g - hat * jnp.mean(g * hat, axis=-1, keepdims=True))
            ).astype(bf16)

        send_out(1, dqs, dq)

        return carry

    lax.fori_loop(0, 8, unit, 0)

    def key_gain(t, carry):
        p, b = t // 16, t % 16
        raw = kv[p, 0, b // SIDE, b % SIDE].astype(f32)
        inv = lax.rsqrt(jnp.mean(raw * raw, axis=-1, keepdims=True) + EPS)
        gacc[1] += fold(dka[p, cols(b * BLK, BLK), :] * (raw * inv), jnp.sum)
        return carry

    lax.fori_loop(0, 32, key_gain, 0)

    g_sends = []
    stages = ((dp, ROWS), (x, SIDE), (y, SIDE))

    def gain_send(n, held):
        place, count = stages[n]
        gb[n, place] = held
        for d in range(1, count):
            j = (place + d) % count
            dev = (j, seq) if n == 0 else dev_of(n - 1, j)
            c = remote(gb.at[n, place], gb.at[n, place], s_g.at[n, d], r_g.at[n, place], dev)
            c.start()
            g_sends.append(c)

    def gain_sum(n):
        place, count = stages[n]
        for d in range(1, count):
            blk = gb.at[n, (place + d) % count]
            pltpu.make_async_copy(blk, blk, r_g.at[n, (place + d) % count]).wait()
        held = gb[n, 0]
        for j in range(1, count):
            held = held + gb[n, j]
        return held

    gain_send(
        0,
        jnp.concatenate(
            [jnp.sum(gacc[i], axis=0, keepdims=True) for i in (0, 1)]
            + [jnp.zeros((6, HD), f32)],
            axis=0,
        ),
    )
    gain_send(1, gain_sum(0))

    f_sends = []
    for p in (0, 1):
        other = mine[1 - p]
        me = mine[p]
        for d in (1, 3, 2):
            slot = (other + d) % SIDE
            for i in (0, 1):
                blk = rb.at[p, slot, i]
                pltpu.make_async_copy(blk, blk, r_rs.at[p, i, slot]).wait()
        for dd in (1, 3, 2, 0):
            j = (me + dd) % SIDE
            b = j * SIDE + y if p == 0 else x * SIDE + j
            rows = cols(b * BLK, BLK)
            kgrad = dka[p, rows, :]
            vgrad = dva[p, rows, :]
            for d in (1, 2, 3):
                slot = (other + d) % SIDE
                kgrad = kgrad + rb[p, slot, 0, j].astype(f32)
                vgrad = vgrad + rb[p, slot, 1, j].astype(f32)
            raw = (kv[0, 0, j, y] if p == 0 else kv[1, 0, x, j]).astype(f32)
            inv = lax.rsqrt(jnp.mean(raw * raw, axis=-1, keepdims=True) + EPS)
            hat = raw * inv
            g = kgrad * kg[...]
            fb[p, 0, j] = (inv * (g - hat * jnp.mean(g * hat, axis=-1, keepdims=True))).astype(
                bf16
            )
            fb[p, 1, j] = vgrad.astype(bf16)
            for i, dst in enumerate((dk, dv)):
                place = dst.at[:, cols(p * 512 + me * HD, HD)]
                if dd == 0:
                    pltpu.make_async_copy(fb.at[p, i, j], place, r_f.at[p, i, me]).start()
                else:
                    c = remote(
                        fb.at[p, i, j], place, s_f.at[p, i, dd], r_f.at[p, i, me], dev_of(p, j)
                    )
                    c.start()
                    f_sends.append(c)

    gain_send(2, gain_sum(1))
    held = gain_sum(2)
    tokens = ROWS * SIDE * SIDE * BLK
    qgp[...] = held[0:1] / math.sqrt(tokens * QH)
    kgp[...] = held[1:2] / math.sqrt(tokens * KVH)

    for c in kv_sends + ag_sends + f_sends + g_sends:
        c.wait_send()

    def drain(t, carry):
        i, p, d = t // 6, (t // 3) % 2, t % 3 + 1
        src = os_.at[0, 0]
        pltpu.make_async_copy(src, src, s_out.at[i, p, d]).wait()
        pltpu.make_async_copy(src, src, s_in.at[i, p, d]).wait()
        return carry

    lax.fori_loop(0, 12, drain, 0)

    for p in (0, 1):
        for i in (0, 1):
            for d in (1, 2, 3):
                blk = rb.at[0, 0, 0]
                pltpu.make_async_copy(blk, blk, s_rs.at[p, i, d]).wait()

    def arrive(t, carry):
        i, p, j = t // 8, (t // 4) % 2, t % 4
        place = o.at[:, cols(p * PART + j * OWN, OWN)]
        pltpu.make_async_copy(place, place, r_out.at[i, p, j]).wait()
        return carry

    lax.fori_loop(0, 16, arrive, 0)
    for p in (0, 1):
        for i, dst in enumerate((dk, dv)):
            for j in range(SIDE):
                place = dst.at[:, cols(p * 512 + j * HD, HD)]
                pltpu.make_async_copy(place, place, r_f.at[p, i, j]).wait()


def on_device(q_proj, k_proj, v_proj, q_gain, k_gain, dout, segments):
    rows = q_proj.shape[0]
    ids = segments.reshape(ROWS, SIDE * SIDE, BLK)
    any_ = pl.BlockSpec(memory_space=pl.ANY)
    vmem = pl.BlockSpec(memory_space=pltpu.VMEM)
    dma = pltpu.SemaphoreType.DMA
    length = SIDE * SIDE * BLK
    o, dq, dk, dv, qgp, kgp = pl.pallas_call(
        kernel,
        out_shape=(
            jax.ShapeDtypeStruct((rows, QH * HD), bf16),
            jax.ShapeDtypeStruct((rows, QH * HD), bf16),
            jax.ShapeDtypeStruct((rows, KVH * HD), bf16),
            jax.ShapeDtypeStruct((rows, KVH * HD), bf16),
            jax.ShapeDtypeStruct((1, HD), f32),
            jax.ShapeDtypeStruct((1, HD), f32),
        ),
        in_specs=[any_, any_, any_, any_, vmem, vmem, vmem],
        out_specs=(any_, any_, any_, any_, vmem, vmem),
        scratch_shapes=[
            pltpu.VMEM((2, SIDE, BLK, OWN), bf16),
            pltpu.VMEM((2, SIDE, BLK, OWN), bf16),
            pltpu.VMEM((2, 2, SIDE, SIDE, BLK, HD), bf16),
            pltpu.VMEM((2, length, HD), bf16),
            pltpu.VMEM((2, length, HD), bf16),
            pltpu.VMEM((2, HD, length), bf16),
            pltpu.VMEM((2, HD, length), bf16),
            pltpu.VMEM((2, SIDE, BLK, OWN), bf16),
            pltpu.VMEM((2, SIDE, BLK, OWN), bf16),
            pltpu.VMEM((length, OWN), f32),
            pltpu.VMEM((SIDE, 1, OWN), f32),
            pltpu.VMEM((16, 1, BLK), jnp.int32),
            pltpu.VMEM((2, length, HD), f32),
            pltpu.VMEM((2, length, HD), f32),
            pltpu.VMEM((2, 2, SIDE, SIDE, BLK, HD), bf16),
            pltpu.VMEM((2, SIDE, 2, SIDE, BLK, HD), bf16),
            pltpu.VMEM((2, 2, SIDE, BLK, HD), bf16),
            pltpu.VMEM((2, OWN, HD), bf16),
            pltpu.VMEM((HD, OWN), f32),
            pltpu.VMEM((HD, OWN), f32),
            pltpu.VMEM((2, 8, HD), f32),
            pltpu.VMEM((3, ROWS, 8, HD), f32),
            dma((2, 2, SIDE)), dma((2, 2, SIDE)),
            dma((2, 2, SIDE)), dma((2, 2, SIDE)),
            dma((2, 2, SIDE)), dma((2, 2, SIDE)),
            dma((2, 2, SIDE)), dma((2, 2, SIDE)),
            dma((2, 2, SIDE)), dma((2, 2, SIDE)),
            dma((2, 2, SIDE)), dma((2, 2, SIDE)),
            dma((3, ROWS)), dma((3, ROWS)),
        ],
        name="exchange_attend",
        cost_estimate=pl.CostEstimate(
            flops=20_000_000_000, bytes_accessed=20_000_000, transcendentals=10_000_000
        ),
        compiler_params=pltpu.CompilerParams(
            collective_id=0, has_side_effects=True, vmem_limit_bytes=58 << 20
        ),
    )(q_proj, k_proj, v_proj, dout, ids, q_gain.reshape(1, HD), k_gain.reshape(1, HD))
    return o, dq, dk, dv, qgp.reshape(HD), kgp.reshape(HD)


def solution(mesh):
    split = P(("dp", "seq"), None)
    return jax.shard_map(
        on_device,
        mesh=mesh,
        in_specs=(split, split, split, P(), P(), split, P()),
        out_specs=(split, split, split, split, P(), P()),
        check_vma=False,
    )
```
